512 devices in a mesh: dp: 32 (over y, z_lo), head: 16 (over z_hi, x, core).
Axes of the slice: x: 4, y: 4, z: 16 (z_hi: 2, z_lo: 8; z = z_hi * 8 + z_lo), core: 2. Of those that a mesh axis runs over, the one named last changes fastest.
Arguments:
- task_embed: bfloat16 [240, 1024], replicated, may hold values from -6 to 6
- task_ids: int32 [64], P('dp'), may hold values from 0 to 239
- seq_lengths: int32 [64], P('dp'), may hold values from 1 to 320, 12800 in all
- w_in: bfloat16 [1024, 256], replicated, may hold values from -0.1875 to 0.1875
- module_embed: float32 [2, 256], replicated, may hold values from -4 to 4
- wa_q: bfloat16 [256, 8, 4096], P('dp', None, 'head'), may hold values from -0.005859375 to 0.005859375
- wb_q: bfloat16 [256, 8, 4096], P('dp', None, 'head'), may hold values from -0.125 to 0.125
- wa_v: bfloat16 [256, 8, 4096], P('dp', None, 'head'), may hold values from -0.005859375 to 0.005859375
- wb_v: bfloat16 [256, 8, 1024], P('dp', None, 'head'), may hold values from -0.125 to 0.125
- base_q: bfloat16 [4096, 4096], P(None, 'head'), may hold values from -0.09375 to 0.09375
- base_v: bfloat16 [4096, 1024], P(None, 'head'), may hold values from -0.09375 to 0.09375
- hidden_in: bfloat16 [64, 320, 4096], P('dp', None, 'head'), may hold values from -6 to 6
- grad_q: bfloat16 [64, 320, 4096], P('dp', None, 'head'), may hold values from -6 to 6
- grad_v: bfloat16 [64, 320, 1024], P('dp', None, 'head'), may hold values from -6 to 6
Outputs:
- q_out: bfloat16 [64, 320, 4096], P('dp', None, 'head')
- v_out: bfloat16 [64, 320, 1024], P('dp', None, 'head')
- grad_wa_q: float32 [256, 8, 4096], P('dp', None, 'head')
- grad_wb_q: float32 [256, 8, 4096], P('dp', None, 'head')
- grad_wa_v: float32 [256, 8, 4096], P('dp', None, 'head')
- grad_wb_v: float32 [256, 8, 1024], P('dp', None, 'head')
- grad_w_in: float32 [1024, 256], P(None, 'dp')
- grad_module: float32 [2, 256], P(None, 'dp')
The draws below stay inside these ranges and needn't reach their ends.
Inputs may be any that keep to these rules, and one draw needn't show every extreme that they name: `seq_lengths`: each task batch holds 1 to 320 real tokens followed by padding; some batch is full.
All inputs are finite; a program needn't handle non-finite values. No bound on the sum of `seq_lengths` on one device may be relied on, other than what follows from the above.
Results may differ from the reference program's by a relative error of at most 0.02.
Values may be sent and summed in bfloat16 or wider, within the bound.
No kernel may reach another device: no remote copies, remote signals or barrier semaphores. Data moves between devices by JAX's collectives and lax.ppermute only.
A program may use at most 64 MiB of HBM per device.

```python
import math
import jax
import jax.numpy as jnp
import numpy as np
from jax import lax

D = 4096
KV = 1024
R = 8
H = 256
E = 1024
TASKS = 240
LEN = 320
SEQS = 64


def set_ends(drawn, stream_key, low, top_value):
    index_at = [jax.random.randint(jax.random.fold_in(stream_key, axis), (), 0, length) for axis, length in enumerate(drawn.shape)]
    main_axis = drawn.shape.index(max(drawn.shape))
    neighbour = index_at[:main_axis] + [(index_at[main_axis] + 1) % drawn.shape[main_axis]] + index_at[main_axis + 1:]
    return drawn.at[tuple(index_at)].set(low).at[tuple(neighbour)].set(top_value)


def steps_of(rng, shape, cuts, low, high):
    def one(dim, shards_of):
        heights = jax.random.uniform(jax.random.fold_in(jax.random.fold_in(rng, 6), dim), (shards_of,), jnp.float32, low / len(cuts), high / len(cuts))
        return jnp.repeat(jnp.exp(heights), shape[dim] // shards_of).reshape((-1,) + (1,) * (len(shape) - dim - 1))

    factor_of = one(*cuts[0])
    for cut in cuts[1:]:
        factor_of = factor_of * one(*cut)
    return factor_of


def profile(amount, total, most, slope):
    weights = [(1 << 20) // math.isqrt(grade ** slope) + 1 for grade in range(2, amount + 1)]
    spare, given = total - most - (amount - 1), [1] * (amount - 1)
    while spare > 0:
        movable = [i for i in range(amount - 1) if given[i] < most]
        pool, left = sum([weights[i] for i in movable]), spare
        for i in movable:
            more = min(most - given[i], max(1, left * weights[i] // pool), spare)
            given[i] = given[i] + more
            spare = spare - more
    return np.array([most] + given)


def uneven_parts(rng, number_of, total, bound, lean):
    if number_of == 2:
        one = jax.random.randint(rng, (), max(1, total - bound), min(bound, total - 1) + 1)
        return jnp.stack([one, total - one])
    lengths = jnp.asarray(profile(number_of, total, bound, lean), jnp.int32)
    couples = (number_of - 1) // 2
    donor, receiver = lengths[1:1 + 2 * couples:2], lengths[2:2 + 2 * couples:2]
    margin = jnp.minimum(donor - 1, bound - receiver)
    moved = jax.random.randint(jax.random.fold_in(rng, 1), (couples,), 0, 1 << 20) % (margin + 1)
    lengths = lengths.at[1:1 + 2 * couples:2].set(donor - moved).at[2:2 + 2 * couples:2].set(receiver + moved)
    return lengths[jax.random.permutation(jax.random.fold_in(rng, 2), number_of)]


def scatter_about(own_key, shape, deviation, bound, split=(), held_as=jnp.bfloat16):
    gain = steps_of(own_key, shape, split, -0.22, 0.18) if split else 1.0
    values = jax.random.normal(own_key, shape, jnp.float32) * deviation * gain
    return jnp.minimum(jnp.maximum(values, -bound), bound).astype(held_as)


def setup_inputs(seed: int = 0) -> dict:
    splits = jax.random.split(jax.random.key(seed), 15)
    return {
        "task_embed": scatter_about(splits[0], (TASKS, E), 1.0, 6.0),
        "task_ids": set_ends(jax.random.randint(splits[1], (SEQS,), 0, TASKS), jax.random.fold_in(splits[1], 1), 0, TASKS - 1).astype(jnp.int32),
        "seq_lengths": uneven_parts(splits[2], SEQS, SEQS * LEN * 5 // 8, LEN, 2).astype(jnp.int32),
        "w_in": scatter_about(splits[3], (E, H), E ** -0.5, 0.1875),
        "module_embed": scatter_about(splits[4], (2, H), 1.0, 4.0, (), jnp.float32),
        "wa_q": scatter_about(splits[5], (H, R, D), (H * D) ** -0.5, 0.005859375, ((0, 32), (2, 16))),
        "wb_q": scatter_about(splits[6], (H, R, D), (H * R) ** -0.5, 0.125, ((0, 32), (2, 16))),
        "wa_v": scatter_about(splits[7], (H, R, D), (H * D) ** -0.5, 0.005859375, ((0, 32), (2, 16))),
        "wb_v": scatter_about(splits[8], (H, R, KV), (H * R) ** -0.5, 0.125, ((0, 32), (2, 16))),
        "base_q": scatter_about(splits[9], (D, D), D ** -0.5, 0.09375, ((1, 16),)),
        "base_v": scatter_about(splits[10], (D, KV), D ** -0.5, 0.09375, ((1, 16),)),
        "hidden_in": scatter_about(splits[11], (SEQS, LEN, D), 1.0, 6.0, ((0, 32), (2, 16))),
        "grad_q": scatter_about(splits[12], (SEQS, LEN, D), 1.0, 6.0, ((0, 32), (2, 16))),
        "grad_v": scatter_about(splits[13], (SEQS, LEN, KV), 1.0, 6.0, ((0, 32), (2, 16))),
    }


def silu_grad(pre):
    sig = jax.nn.sigmoid(pre)
    return sig * (1.0 + pre * (1.0 - sig))

def one_batch(hidden, a_q, query_up_factor, a_v, value_up_factor, cot_q, cot_v, length, base_q, base_v):
    query_down_product = jnp.dot(hidden, a_q.T, preferred_element_type=jnp.float32).astype(jnp.bfloat16)
    value_down_product = jnp.dot(hidden, a_v.T, preferred_element_type=jnp.float32).astype(jnp.bfloat16)
    q_out = (jnp.dot(hidden, base_q, preferred_element_type=jnp.float32) + 2.0 * jnp.dot(query_down_product, query_up_factor, preferred_element_type=jnp.float32)).astype(jnp.bfloat16)
    v_out = (jnp.dot(hidden, base_v, preferred_element_type=jnp.float32) + 2.0 * jnp.dot(value_down_product, value_up_factor, preferred_element_type=jnp.float32)).astype(jnp.bfloat16)
    positions = jnp.arange(hidden.shape[0], dtype=jnp.int32)
    weight = (positions < length).astype(jnp.float32) / length.astype(jnp.float32)
    query_output_gradient = (cot_q.astype(jnp.float32) * weight[:, None]).astype(jnp.bfloat16)
    value_output_gradient = (cot_v.astype(jnp.float32) * weight[:, None]).astype(jnp.bfloat16)
    query_up_gradient = 2.0 * jnp.dot(query_down_product.T, query_output_gradient, preferred_element_type=jnp.float32)
    value_up_gradient = 2.0 * jnp.dot(value_down_product.T, value_output_gradient, preferred_element_type=jnp.float32)
    du_q = (2.0 * jnp.dot(query_output_gradient, query_up_factor.T, preferred_element_type=jnp.float32)).astype(jnp.bfloat16)
    du_v = (2.0 * jnp.dot(value_output_gradient, value_up_factor.T, preferred_element_type=jnp.float32)).astype(jnp.bfloat16)
    d_aq = jnp.dot(du_q.T, hidden, preferred_element_type=jnp.float32)
    d_av = jnp.dot(du_v.T, hidden, preferred_element_type=jnp.float32)
    return (q_out, v_out, d_aq, query_up_gradient, d_av, value_up_gradient)

def reference(task_embed, task_ids, seq_lengths, w_in, module_embed, wa_q, wb_q, wa_v, wb_v, base_q, base_v, hidden_in, grad_q, grad_v):
    highest = lax.Precision.HIGHEST
    onehot = (task_ids[:, None] == jnp.arange(TASKS, dtype=jnp.int32)[None, :]).astype(jnp.bfloat16)
    embeds = jnp.dot(onehot, task_embed, preferred_element_type=jnp.float32)
    pre = jnp.dot(embeds.astype(jnp.bfloat16), w_in, preferred_element_type=jnp.float32)[:, None, :] + module_embed[None, :, :]
    latent = lax.optimization_barrier(jax.nn.silu(pre).astype(jnp.bfloat16))
    lat32 = latent.astype(jnp.float32)

    def make(lat, weights):
        return jnp.einsum('sh,hrc->src', lat, weights.astype(jnp.float32)).astype(jnp.bfloat16)
    a_q = make(lat32[:, 0], wa_q)
    query_up_factor = make(lat32[:, 0], wb_q)
    a_v = make(lat32[:, 1], wa_v)
    value_up_factor = make(lat32[:, 1], wb_v)

    def per_batch(items):
        return one_batch(items[0], items[1], items[2], items[3], items[4], items[5], items[6], items[7], base_q, base_v)
    q_out, v_out, d_aq, query_up_gradient, d_av, value_up_gradient = lax.map(per_batch, (hidden_in, a_q, query_up_factor, a_v, value_up_factor, grad_q, grad_v, seq_lengths))
    grad_wa_q = jnp.einsum('sh,src->hrc', lat32[:, 0], d_aq, precision=highest)
    grad_wb_q = jnp.einsum('sh,src->hrc', lat32[:, 0], query_up_gradient, precision=highest)
    grad_wa_v = jnp.einsum('sh,src->hrc', lat32[:, 1], d_av, precision=highest)
    grad_wb_v = jnp.einsum('sh,src->hrc', lat32[:, 1], value_up_gradient, precision=highest)
    d_query = jnp.einsum('src,hrc->sh', d_aq, wa_q.astype(jnp.float32), precision=highest) + jnp.einsum('src,hrc->sh', query_up_gradient, wb_q.astype(jnp.float32), precision=highest)
    d_value = jnp.einsum('src,hrc->sh', d_av, wa_v.astype(jnp.float32), precision=highest) + jnp.einsum('src,hrc->sh', value_up_gradient, wb_v.astype(jnp.float32), precision=highest)
    d_latent = jnp.stack([d_query, d_value], axis=1)
    d_pre = d_latent * silu_grad(pre)
    grad_w_in = jnp.dot(embeds.T, d_pre[:, 0] + d_pre[:, 1], precision=highest)
    grad_module = lax.optimization_barrier(jnp.sum(d_pre, axis=0))
    return (q_out, v_out, grad_wa_q, grad_wb_q, grad_wa_v, grad_wb_v, grad_w_in, grad_module)
```

```python
import jax
import jax.numpy as jnp
from jax import lax
from jax.sharding import Mesh, PartitionSpec as P

bf16, f32 = jnp.bfloat16, jnp.float32
scale = 2.0


def silu_grad(pre):
    sig = jax.nn.sigmoid(pre)
    return sig * (1.0 + pre * (1.0 - sig))


def swap(blocks, axes):
    return lax.all_to_all(blocks, axes, 0, 0, tiled=True)


def spread(block, axes, n):
    return swap(jnp.broadcast_to(block[None], (n,) + block.shape), axes)


def dot(eq, a, b):
    return jnp.einsum(eq, a, b, preferred_element_type=f32)


def on_device(
    task_embed,
    task_ids,
    seq_lengths,
    w_in,
    module_embed,
    wa_q,
    wb_q,
    wa_v,
    wb_v,
    base_q,
    base_v,
    hidden_in,
    grad_q,
    grad_v,
):
    ny, nz, nh, nx, nc = (lax.axis_size(a) for a in ("y", "zl", "zh", "x", "c"))
    y, zl, zh = (lax.axis_index(a) for a in ("y", "zl", "zh"))
    xc = ("x", "c")
    head = ("zh", "x", "c")
    seqs, length, wq = hidden_in.shape
    rows, rank, _ = wa_q.shape
    wv = wb_v.shape[2]
    tasks = task_embed.shape[0]
    split, width = 2 * wq, 3 * wq + wv

    other = lax.ppermute(hidden_in, "zh", [(0, 1), (1, 0)])
    near = lax.all_gather(hidden_in, xc, axis=0, tiled=False)
    far = lax.all_gather(other, xc, axis=0, tiled=False)

    ids_near = spread(jnp.broadcast_to(task_ids[:, None], (seqs, 128)), "zl", nz)[:, :, 0].reshape(-1)
    packed = jnp.concatenate([wa_q, wb_q, wa_v, wb_v], axis=2)
    w_y = spread(packed, "y", ny)

    pre_t = lax.dot_general(w_in, task_embed, (((0,), (1,)), ((), ())), preferred_element_type=f32)
    pre_t = pre_t[None] + module_embed[:, :, None]
    pre_z = lax.dynamic_slice_in_dim(pre_t.reshape(2, ny, nz, rows, tasks), zl, 1, 2)[:, :, 0]
    lat_z = jax.nn.silu(pre_z).astype(bf16).reshape(2, ny * rows, tasks)
    pre_own = lax.dynamic_slice_in_dim(pre_z, y, 1, 1)[:, 0]
    lat_own = jax.nn.silu(pre_own).astype(bf16)
    sg_own = silu_grad(pre_own)

    def picked(ids):
        return (jnp.arange(tasks, dtype=jnp.int32)[:, None] == ids[None, :]).astype(bf16)

    lat_near = dot("mht,ts->mhs", lat_z, picked(ids_near)).astype(bf16)
    w_all = w_y.reshape(ny * rows, rank, width)
    part = jnp.concatenate(
        [
            dot("hs,hrc->src", lat_near[0], w_all[:, :, :split]),
            dot("hs,hrc->src", lat_near[1], w_all[:, :, split:]),
        ],
        axis=2,
    ).astype(bf16)
    got = swap(part.reshape(nz, seqs * rank, width), "zl")
    adapters = jnp.sum(got.astype(f32), axis=0).astype(bf16).reshape(seqs, rank, width)
    a_q, b_q = adapters[:, :, :wq], adapters[:, :, wq:split]
    a_v, b_v = adapters[:, :, split : split + wq], adapters[:, :, split + wq :]

    positions = jnp.arange(length, dtype=jnp.int32)
    weight = (positions[None, :] < seq_lengths[:, None]).astype(f32) / seq_lengths.astype(f32)[:, None]
    w2 = scale * weight[:, None, :]
    u_q = dot("srd,std->srt", a_q, hidden_in)
    u_v = dot("srd,std->srt", a_v, hidden_in)
    du_q = dot("src,stc->srt", b_q, grad_q) * w2
    du_v = dot("src,stc->srt", b_v, grad_v) * w2
    low = jnp.stack([u_q, u_v, du_q, du_v], axis=1).astype(bf16)
    low = swap(low.reshape(nx * nc, rank, length), xc)
    low = jnp.sum(low.astype(f32), axis=0).astype(bf16)
    low = spread(low, head, nh * nx * nc)
    low = jnp.sum(low.reshape(nh, seqs, 4, rank, length).astype(f32), axis=0)
    u32 = low[:, :2]
    u = u32.astype(bf16)
    ug = (u32 * w2[:, None]).astype(bf16)
    du = low[:, 2:].astype(bf16)
    d_a = dot("smrt,std->smrd", du, hidden_in)
    d_bq = dot("srt,stc->src", ug[:, 0], grad_q)
    d_bv = dot("srt,stc->src", ug[:, 1], grad_v)
    ids_col = jnp.broadcast_to(task_ids.astype(f32)[:, None, None], (seqs, rank, 64))
    d_own = jnp.concatenate([d_a[:, 0], d_bq, d_a[:, 1], d_bv, ids_col], axis=2).astype(bf16)
    d_z = spread(d_own.reshape(seqs * rank, width + 64), "zl", nz)
    d_all = spread(d_z.reshape(nz * seqs * rank, width + 64), "y", ny)
    d_all = d_all.reshape(ny * nz * seqs, rank, width + 64)

    ids_all = d_all[:, 0, width].astype(jnp.int32)
    pick_all = picked(ids_all)
    lat_all = dot("mht,ts->mhs", lat_own, pick_all).astype(bf16)
    d_q, d_v = d_all[:, :, :split], d_all[:, :, split:width]
    grads_q = dot("hs,src->hrc", lat_all[0], d_q)
    grads_v = dot("hs,src->hrc", lat_all[1], d_v)
    d_lat = jnp.stack(
        [dot("src,hrc->hs", d_q, packed[:, :, :split]), dot("src,hrc->hs", d_v, packed[:, :, split:])]
    )
    d_lat = spread(d_lat.reshape(2 * rows, -1), head, nh * nx * nc)
    d_lat = jnp.sum(d_lat, axis=0).reshape(2, rows, -1)
    sg_all = jnp.einsum("mht,ts->mhs", sg_own, pick_all.astype(f32), precision=lax.Precision.HIGHEST)
    d_pre = d_lat * sg_all
    embeds = dot("ts,te->se", pick_all, task_embed).astype(bf16)
    both = d_pre[0] + d_pre[1]
    hi = both.astype(bf16)
    lo = (both - hi.astype(f32)).astype(bf16)
    grad_in = dot("se,hs->eh", embeds, hi) + dot("se,hs->eh", embeds, lo)
    grad_mod = jnp.sum(d_pre, axis=2)

    cols = nx * nc
    base_q = base_q.reshape(nh, cols, wq, -1)
    base_v = base_v.reshape(nh, cols, wq, -1)
    full = jnp.stack([jnp.where(zh == 0, near, far), jnp.where(zh == 0, far, near)])
    q_out = dot("gjstd,gjdc->stc", full, base_q) + scale * dot("srt,src->stc", u[:, 0], b_q)
    v_out = dot("gjstd,gjdc->stc", full, base_v) + scale * dot("srt,src->stc", u[:, 1], b_v)

    return (
        q_out.astype(bf16),
        v_out.astype(bf16),
        grads_q[:, :, :wq],
        grads_q[:, :, wq:],
        grads_v[:, :, :wq],
        grads_v[:, :, wq:],
        grad_in,
        grad_mod,
    )


def solution(mesh):
    fine = Mesh(mesh.devices.reshape(4, 8, 2, 4, 2), ("y", "zl", "zh", "x", "c"))
    dp, head = ("y", "zl"), ("zh", "x", "c")
    rows_cols = P(dp, None, head)
    return jax.shard_map(
        on_device,
        mesh=fine,
        in_specs=(P(), P(dp), P(dp), P(), P())
        + (rows_cols,) * 4
        + (P(None, head),) * 2
        + (rows_cols,) * 3,
        out_specs=(rows_cols,) * 6 + (P(None, dp),) * 2,
        check_vma=False,
    )
```

```python
import jax
import jax.numpy as jnp
from jax import lax
from jax.experimental import pallas as pl
from jax.experimental.pallas import tpu as pltpu
from jax.sharding import Mesh, PartitionSpec as P

bf16, f32 = jnp.bfloat16, jnp.float32
scale = 2.0


def silu_grad(pre):
    sig = jax.nn.sigmoid(pre)
    return sig * (1.0 + pre * (1.0 - sig))


def swap(blocks, axes):
    return lax.all_to_all(blocks, axes, 0, 0, tiled=True)


def spread(block, axes, n):
    return swap(jnp.broadcast_to(block[None], (n,) + block.shape), axes)


def dot(eq, a, b):
    return jnp.einsum(eq, a, b, preferred_element_type=f32)


def base_kernel(order, *refs):
    near = refs[:8]
    base_q, base_vt, u, ad, q_out, vt_out, acc_q, acc_v = refs[8:]
    seqs, length, wq = q_out.shape
    wv = vt_out.shape[1]
    for n, block in enumerate(near):
        for half in range(2):
            h = block[half].reshape(seqs * length, wq)
            at = pl.ds(pl.multiple_of(order[2 * n + half] * wq, wq), wq)
            add_q = jnp.dot(h, base_q[at, :], preferred_element_type=f32)
            add_v = lax.dot_general(h, base_vt[:, at], (((1,), (1,)), ((), ())), preferred_element_type=f32)
            if n + half == 0:
                acc_q[...], acc_v[...] = add_q, add_v
            else:
                acc_q[...] += add_q
                acc_v[...] += add_v
    first = (((0,), (0,)), ((), ()))
    for s in range(seqs):
        own = slice(s * length, (s + 1) * length)
        b_q, b_v = ad[s, :, wq : 2 * wq], ad[s, :, 3 * wq : 3 * wq + wv]
        low_q = lax.dot_general(u[s, 0], b_q, first, preferred_element_type=f32)
        low_v = lax.dot_general(b_v, u[s, 1], first, preferred_element_type=f32)
        q_out[s] = (acc_q[own, :] + scale * low_q).astype(bf16)
        vt_out[s] = (acc_v[own, :].T + scale * low_v).astype(bf16)


def base_product(order, blocks, base_q, base_vt, u, adapters, wv):
    _, seqs, length, wq = blocks[0].shape
    in_vmem = pl.BlockSpec(memory_space=pltpu.VMEM)
    return pl.pallas_call(
        base_kernel,
        out_shape=(
            jax.ShapeDtypeStruct((seqs, length, wq), bf16),
            jax.ShapeDtypeStruct((seqs, wv, length), bf16),
        ),
        in_specs=[pl.BlockSpec(memory_space=pltpu.SMEM)] + [in_vmem] * (len(blocks) + 4),
        out_specs=(in_vmem, in_vmem),
        scratch_shapes=[pltpu.VMEM((seqs * length, wq), f32), pltpu.VMEM((seqs * length, wv), f32)],
        compiler_params=pltpu.CompilerParams(vmem_limit_bytes=32 * 2**20),
        cost_estimate=pl.CostEstimate(flops=2_000_000_000, bytes_accessed=9_000_000, transcendentals=0),
        name="base_product",
    )(order, *blocks, base_q, base_vt, u, adapters)


def on_device(
    task_embed,
    task_ids,
    seq_lengths,
    w_in,
    module_embed,
    wa_q,
    wb_q,
    wa_v,
    wb_v,
    base_q,
    base_v,
    hidden_in,
    grad_q,
    grad_v,
):
    ny, nz, nh, nx, nc = (lax.axis_size(a) for a in ("y", "zl", "zh", "x", "c"))
    y, zl, zh = (lax.axis_index(a) for a in ("y", "zl", "zh"))
    xc = ("x", "c")
    head = ("zh", "x", "c")
    seqs, length, wq = hidden_in.shape
    rows, rank, _ = wa_q.shape
    wv = wb_v.shape[2]
    tasks = task_embed.shape[0]
    split, width = 2 * wq, 3 * wq + wv

    other = lax.ppermute(hidden_in, "zh", [(0, 1), (1, 0)])

    ids_near = spread(jnp.broadcast_to(task_ids[:, None], (seqs, 128)), "zl", nz)[:, :, 0].reshape(-1)
    packed = jnp.concatenate([wa_q, wb_q, wa_v, wb_v], axis=2)
    w_y = lax.all_gather(packed, "y", axis=0, tiled=False)

    pre_t = lax.dot_general(w_in, task_embed, (((0,), (1,)), ((), ())), preferred_element_type=f32)
    pre_t = pre_t[None] + module_embed[:, :, None]
    pre_z = lax.dynamic_slice_in_dim(pre_t.reshape(2, ny, nz, rows, tasks), zl, 1, 2)[:, :, 0]
    lat_z = jax.nn.silu(pre_z).astype(bf16).reshape(2, ny * rows, tasks)
    pre_own = lax.dynamic_slice_in_dim(pre_z, y, 1, 1)[:, 0]
    lat_own = jax.nn.silu(pre_own).astype(bf16)
    sg_own = silu_grad(pre_own)

    def picked(ids):
        return (jnp.arange(tasks, dtype=jnp.int32)[:, None] == ids[None, :]).astype(bf16)

    lat_near = dot("mht,ts->mhs", lat_z, picked(ids_near)).astype(bf16)
    w_all = w_y.reshape(ny * rows, rank, width)
    part = jnp.concatenate(
        [
            dot("hs,hrc->src", lat_near[0], w_all[:, :, :split]),
            dot("hs,hrc->src", lat_near[1], w_all[:, :, split:]),
        ],
        axis=2,
    ).astype(bf16)
    got = swap(part.reshape(nz, seqs * rank, width), "zl")
    got, other = lax.optimization_barrier((got, other))
    both_z = jnp.stack([hidden_in, other])
    turned = [both_z] + [lax.ppermute(both_z, "x", [(i, (i + k) % nx) for i in range(nx)]) for k in range(1, nx)]
    adapters = jnp.sum(got.astype(f32), axis=0).astype(bf16).reshape(seqs, rank, width)
    a_q, b_q = adapters[:, :, :wq], adapters[:, :, wq:split]
    a_v, b_v = adapters[:, :, split : split + wq], adapters[:, :, split + wq :]

    positions = jnp.arange(length, dtype=jnp.int32)
    weight = (positions[None, :] < seq_lengths[:, None]).astype(f32) / seq_lengths.astype(f32)[:, None]
    w2 = scale * weight[:, None, :]
    u_q = dot("srd,std->srt", a_q, hidden_in)
    u_v = dot("srd,std->srt", a_v, hidden_in)
    du_q = dot("src,stc->srt", b_q, grad_q) * w2
    du_v = dot("src,stc->srt", b_v, grad_v) * w2
    low = jnp.stack([u_q, u_v, du_q, du_v], axis=1).astype(bf16)
    low = swap(low.reshape(nx * nc, rank, length), xc)
    low = jnp.sum(low.astype(f32), axis=0).astype(bf16)
    low = spread(low, head, nh * nx * nc)
    low = jnp.sum(low.reshape(nh, seqs, 4, rank, length).astype(f32), axis=0)
    u32 = low[:, :2]
    u = u32.astype(bf16)
    ug = (u32 * w2[:, None]).astype(bf16)
    du = low[:, 2:].astype(bf16)
    d_a = dot("smrt,std->smrd", du, hidden_in)
    d_bq = dot("srt,stc->src", ug[:, 0], grad_q)
    d_bv = dot("srt,stc->src", ug[:, 1], grad_v)
    turned = turned + [lax.ppermute(t, "c", [(0, 1), (1, 0)]) for t in turned]
    ids_col = jnp.broadcast_to(task_ids.astype(f32)[:, None, None], (seqs, rank, 64))
    d_own = jnp.concatenate([d_a[:, 0], d_bq, d_a[:, 1], d_bv, ids_col], axis=2).astype(bf16)
    d_z = spread(d_own.reshape(seqs * rank, width + 64), "zl", nz)
    d_all = spread(d_z.reshape(nz * seqs * rank, width + 64), "y", ny)
    d_all = d_all.reshape(ny * nz * seqs, rank, width + 64)

    ids_all = d_all[:, 0, width].astype(jnp.int32)
    pick_all = picked(ids_all)
    lat_all = dot("mht,ts->mhs", lat_own, pick_all).astype(bf16)
    d_q, d_v = d_all[:, :, :split], d_all[:, :, split:width]
    grads_q = dot("hs,src->hrc", lat_all[0], d_q)
    grads_v = dot("hs,src->hrc", lat_all[1], d_v)
    d_lat = jnp.stack(
        [dot("src,hrc->hs", d_q, packed[:, :, :split]), dot("src,hrc->hs", d_v, packed[:, :, split:])]
    )
    batches = d_lat.shape[2]
    d_lat = jnp.pad(d_lat.reshape(2 * rows, batches), ((0, 0), (0, 128 - batches)))
    d_lat = spread(d_lat, head, nh * nx * nc)
    sg_all = jnp.einsum("mht,ts->mhs", sg_own, pick_all.astype(f32), precision=lax.Precision.HIGHEST)
    embeds = dot("ts,te->se", pick_all, task_embed).astype(bf16)

    x, c = lax.axis_index("x"), lax.axis_index("c")
    order = jnp.stack(
        [
            (zh ^ half) * (nx * nc) + lax.rem(x - k + nx, nx) * nc + (c ^ core)
            for core in range(nc)
            for k in range(nx)
            for half in range(nh)
        ]
    ).astype(jnp.int32)
    q_out, vt_out = base_product(order, turned, base_q, base_v.T, u, adapters, wv)
    d_lat, sg_all, embeds, q_out, vt_out, grads_q, grads_v = lax.optimization_barrier(
        (d_lat, sg_all, embeds, q_out, vt_out, grads_q, grads_v)
    )
    d_lat = jnp.sum(d_lat, axis=0)[:, :batches].reshape(2, rows, batches)
    d_pre = d_lat * sg_all
    both = d_pre[0] + d_pre[1]
    hi = both.astype(bf16)
    lo = (both - hi.astype(f32)).astype(bf16)
    grad_in = dot("se,hs->eh", embeds, hi) + dot("se,hs->eh", embeds, lo)
    grad_mod = jnp.sum(d_pre, axis=2)

    return (
        q_out,
        vt_out.swapaxes(1, 2),
        grads_q[:, :, :wq],
        grads_q[:, :, wq:],
        grads_v[:, :, :wq],
        grads_v[:, :, wq:],
        grad_in,
        grad_mod,
    )


def solution(mesh):
    fine = Mesh(mesh.devices.reshape(4, 8, 2, 4, 2), ("y", "zl", "zh", "x", "c"))
    dp, head = ("y", "zl"), ("zh", "x", "c")
    rows_cols = P(dp, None, head)
    return jax.shard_map(
        on_device,
        mesh=fine,
        in_specs=(P(), P(dp), P(dp), P(), P())
        + (rows_cols,) * 4
        + (P(None, head),) * 2
        + (rows_cols,) * 3,
        out_specs=(rows_cols,) * 6 + (P(None, dp),) * 2,
        check_vma=False,
    )
```

```python
import functools

import jax
import jax.numpy as jnp
from jax import lax
from jax.experimental import pallas as pl
from jax.experimental.pallas import tpu as pltpu
from jax.sharding import Mesh, PartitionSpec as P

bf16, f32 = jnp.bfloat16, jnp.float32
exact = lax.Precision.HIGHEST
scale = 2.0


def mm(a, b, dims=((1,), (0,)), precision=None):
    return lax.dot_general(a, b, (dims, ((), ())), precision=precision, preferred_element_type=f32)


def mm_nt(a, b, precision=None):
    return mm(a, b, ((1,), (1,)), precision)


def iota(shape, dim):
    return lax.broadcasted_iota(jnp.int32, shape, dim)


def silu_grad(pre):
    sig = jax.nn.sigmoid(pre)
    return sig * (1.0 + pre * (1.0 - sig))


def swap(blocks, axes):
    return lax.all_to_all(blocks, axes, 0, 0, tiled=True)


def spread(block, axes, n):
    return swap(jnp.broadcast_to(block[None], (n,) + block.shape), axes)


def local(body, outs, args, scalars=0, scratch=(), flops=1_000_000, name=None):
    in_vmem = pl.BlockSpec(memory_space=pltpu.VMEM)
    in_smem = pl.BlockSpec(memory_space=pltpu.SMEM)
    return pl.pallas_call(
        body,
        out_shape=tuple(jax.ShapeDtypeStruct(s, d) for s, d in outs),
        in_specs=[in_smem] * scalars + [in_vmem] * (len(args) - scalars),
        out_specs=tuple(in_vmem for _ in outs),
        scratch_shapes=list(scratch),
        compiler_params=pltpu.CompilerParams(vmem_limit_bytes=32 * 2**20),
        cost_estimate=pl.CostEstimate(flops=flops, bytes_accessed=100_000, transcendentals=0),
        name=name,
    )(*args)


def tables_kernel(ny, nz, place, task_embed, w_in, module, lat_line, lat_own, sg_own):
    latents = w_in.shape[1]
    rows = latents // (ny * nz)
    rank = lat_own.shape[2] // rows
    y, z = place[0], place[1]
    pre = mm(task_embed[...], w_in[...])
    q = iota((latents, lat_line.shape[2]), 1)
    line = iota((latents, lat_line.shape[2]), 0) == (
        (q // (rows * rank)) * (nz * rows) + z * rows + (q // rank) % rows
    )
    line = line.astype(f32).astype(bf16)
    first = (y * nz + z) * rows
    q = iota((latents, lat_own.shape[2]), 1)
    own = (iota((latents, lat_own.shape[2]), 0) == first + q // rank).astype(f32).astype(bf16)
    mine = (iota((rows, latents), 1) == first + iota((rows, latents), 0)).astype(f32)
    for m in range(2):
        p = pre + module[m : m + 1, :]
        lat = (p * jax.nn.sigmoid(p)).astype(bf16)
        lat_line[m] = mm(lat, line).astype(bf16)
        lat_own[m] = mm(lat, own).astype(bf16)
        sg_own[m * rows : (m + 1) * rows, :] = mm_nt(mine, silu_grad(p), exact)


def part_kernel(split, rank, ids, lat_line, w_line, part):
    n, k = part.shape[0], w_line.shape[0]
    tasks = lat_line.shape[1]
    at = ids[...].reshape(n, ids.shape[2])[:, :1]
    pick = (iota((n, tasks), 1) == at).astype(f32).astype(bf16)
    same = iota((n, k), 0) % rank == iota((n, k), 1) % rank
    for m, cols in enumerate((slice(0, split), slice(split, None))):
        spread_lat = jnp.where(same, mm(pick, lat_line[m]), 0.0).astype(bf16)
        part[:, cols] = mm(spread_lat, w_line[:, cols]).astype(bf16)


def row_weight(lengths, s, length):
    n = jnp.full((1, length), lengths[s], jnp.int32)
    return jnp.where(iota((1, length), 1) < n, scale / n.astype(f32), 0.0)


def low_kernel(wq, wv, rank, lengths, got, hidden, grad_q, grad_vt, adapters, low):
    total = got[0].astype(f32)
    for i in range(1, got.shape[0]):
        total += got[i].astype(f32)
    adapters[...] = total.astype(bf16)
    total = total.astype(bf16).astype(f32)
    for s in range(hidden.shape[0]):
        own = total[s * rank : (s + 1) * rank, :]
        a = jnp.concatenate([own[:, :wq], own[:, 2 * wq : 3 * wq]], axis=0).astype(bf16)
        b_q, b_v = own[:, wq : 2 * wq].astype(bf16), own[:, 3 * wq :].astype(bf16)
        low[s, 0] = mm_nt(a, hidden[s])
        back = jnp.concatenate([mm_nt(b_q, grad_q[s]), mm(b_v, grad_vt[s])], axis=0)
        low[s, 1] = back * row_weight(lengths, s, hidden.shape[1])


def adapter_grad_kernel(wq, wv, rank, lengths, ids, low, hidden, grad_q, grad_vt, out, rows):
    for s in range(hidden.shape[0]):
        at = slice(s * rank, (s + 1) * rank)
        weight = row_weight(lengths, s, hidden.shape[1])
        du = jnp.concatenate([low[4 * s + 2], low[4 * s + 3]], axis=0).astype(bf16)
        d_a = mm(du, hidden[s])
        rows[at, :wq] = d_a[:rank]
        rows[at, wq : 2 * wq] = mm((low[4 * s] * weight).astype(bf16), grad_q[s])
        rows[at, 2 * wq : 3 * wq] = d_a[rank:]
        rows[at, 3 * wq : 3 * wq + wv] = mm_nt((low[4 * s + 1] * weight).astype(bf16), grad_vt[s])
        rest = rows.shape[1] - 3 * wq - wv
        rows[at, 3 * wq + wv :] = jnp.full((rank, rest), ids[s], jnp.int32).astype(f32)
    done = rows[...].astype(bf16)
    for i in range(out.shape[0]):
        out[i] = done


def latent_grad_kernel(split, width, rank, d_all, weights, out):
    n, k = d_all.shape[0], weights.shape[0]
    same = iota((n, k), 0) % rank == iota((n, k), 1) % rank
    fold = (iota((k // rank, k), 0) == iota((k // rank, k), 1) // rank).astype(f32)
    parts = []
    for cols in (slice(0, split), slice(split, width)):
        full = jnp.where(same, mm_nt(d_all[:, cols], weights[:, cols]), 0.0)
        by_batch = jnp.sum(full.reshape(n // rank, rank, k), axis=1)
        parts.append(mm_nt(fold, by_batch, exact))
    both = jnp.concatenate(parts, axis=0)
    pad = out.shape[2] - both.shape[1]
    both = jnp.concatenate([both, jnp.zeros((both.shape[0], pad), f32)], axis=1)
    for i in range(out.shape[0]):
        out[i] = both


def head_grad_kernel(wq, wv, rank, d_all, lat_own, sg_own, task_embed, g_aq, g_bq, g_av, g_bv, sg_all, embeds):
    n, k = d_all.shape[0], lat_own.shape[2]
    tasks = lat_own.shape[1]
    width = 3 * wq + wv
    tail = d_all[:, 3 * wq :].astype(f32)
    pick = (iota((n, tasks), 1).astype(f32) == tail[:, wv : wv + 1]).astype(f32)
    same = iota((n, k), 0) % rank == iota((n, k), 1) % rank
    lat = [jnp.where(same, mm(pick.astype(bf16), lat_own[m]), 0.0).astype(bf16) for m in range(2)]
    g_q = mm(lat[0], d_all[:, : 2 * wq], ((0,), (0,)))
    g_aq[...], g_bq[...] = g_q[:, :wq], g_q[:, wq:]
    g_v = mm(lat[1], d_all[:, 2 * wq : width], ((0,), (0,)))
    g_av[...], g_bv[...] = g_v[:, :wq], g_v[:, wq:]
    one = jnp.where(iota((n, tasks), 0) % rank == 0, pick, 0.0)
    one = jnp.sum(one.reshape(n // rank, rank, tasks), axis=1)
    sg_all[...] = mm_nt(sg_own[...], one, exact)
    embeds[...] = mm(one.astype(bf16), task_embed[...]).astype(bf16)


def trunk_kernel(got, sg_all, embeds, g_in, g_mod):
    total = got[0]
    for i in range(1, got.shape[0]):
        total += got[i]
    rows, batches = sg_all.shape
    d_pre = total[:, :batches] * sg_all[...]
    both = d_pre[: rows // 2] + d_pre[rows // 2 :]
    hi = both.astype(bf16)
    lo = (both - hi.astype(f32)).astype(bf16)
    g_in[...] = mm(hi, embeds[...]) + mm(lo, embeds[...])
    g_mod[...] = jnp.sum(d_pre, axis=1, keepdims=True)


def base_kernel(order, *refs):
    near = refs[:8]
    base_q, base_vt, part_q, part_vt, acc_q, acc_v, out = refs[8:]
    seqs, length, wq = near[0].shape
    for n, block in enumerate(near):
        h = block[...].reshape(seqs * length, wq)
        at = pl.ds(pl.multiple_of(order[2 * n] * wq, wq), wq)
        far = pl.ds(pl.multiple_of(order[2 * n + 1] * wq, wq), wq)
        adds = mm(h, base_q[at, :]), mm_nt(h, base_vt[:, at])
        partner = jnp.concatenate([mm(h, part_q[far, :]), mm_nt(h, part_vt[:, far])], axis=1)
        if n == 0:
            acc_q[...], acc_v[...] = adds
            both = partner
        else:
            acc_q[...] += adds[0]
            acc_v[...] += adds[1]
            both += partner
    out[...] = both.astype(bf16)


def out_kernel(rank, acc_q, acc_v, got, low, ad, q_out, vt_out):
    seqs, length, wq = q_out.shape
    both = ad[...].astype(f32)
    first = ((0,), (0,))
    for s in range(seqs):
        own = slice(s * length, (s + 1) * length)
        b = both[s * rank : (s + 1) * rank, :].astype(bf16)
        low_q = mm(low[4 * s].astype(bf16), b[:, wq : 2 * wq], first)
        low_v = mm(b[:, 3 * wq :], low[4 * s + 1].astype(bf16), first)
        got_q, got_v = got[own, :wq].astype(f32), got[own, wq:].astype(f32)
        q_out[s] = (acc_q[own, :] + got_q + scale * low_q).astype(bf16)
        vt_out[s] = ((acc_v[own, :] + got_v).T + scale * low_v).astype(bf16)


def on_device(
    task_embed,
    task_ids,
    seq_lengths,
    w_in,
    module_embed,
    wa_q,
    wb_q,
    wa_v,
    wb_v,
    base_q,
    base_v,
    hidden_in,
    grad_q,
    grad_v,
):
    ny, nz, nh, nx, nc = (lax.axis_size(a) for a in ("y", "zl", "zh", "x", "c"))
    y, zl, zh, x, c = (lax.axis_index(a) for a in ("y", "zl", "zh", "x", "c"))
    xc, head = ("x", "c"), ("zh", "x", "c")
    seqs, length, wq = hidden_in.shape
    rows, rank, _ = wa_q.shape
    wv = wb_v.shape[2]
    tasks, emb = task_embed.shape
    split, width = 2 * wq, 3 * wq + wv
    batches = seqs * ny * nz
    grad_vt = grad_v.swapaxes(1, 2)

    ids_rows = jnp.broadcast_to(task_ids[:, None, None], (seqs, rank, 128)).reshape(seqs * rank, 128)
    ids_line = spread(ids_rows, "zl", nz)
    other = lax.ppermute(hidden_in, "zh", [(0, 1), (1, 0)])
    packed = jnp.concatenate([wa_q, wb_q, wa_v, wb_v], axis=2).reshape(rows * rank, width)
    w_line = lax.all_gather(packed, "y", axis=0, tiled=True)
    lat_line, lat_own, sg_own = local(
        functools.partial(tables_kernel, ny, nz),
        [((2, tasks, ny * rows * rank), bf16), ((2, tasks, rows * rank), bf16), ((2 * rows, tasks), f32)],
        (jnp.stack([y, zl]).astype(jnp.int32), task_embed, w_in, module_embed),
        scalars=1,
        name="tables",
    )
    turns = [[(i, (i + k) % nx) for i in range(nx)] for k in range(1, nx)]
    near = [lax.ppermute(hidden_in, "x", t) for t in turns]
    ids_line, w_line, other, *near = lax.optimization_barrier((ids_line, w_line, other, *near))
    far = [lax.ppermute(other, "x", t) for t in turns]

    (part,) = local(
        functools.partial(part_kernel, split, rank),
        [((nz * seqs * rank, width), bf16)],
        (ids_line, lat_line, w_line),
        name="adapter_parts",
    )
    got = swap(part.reshape(nz, seqs * rank, width), "zl")
    adapters, low = local(
        functools.partial(low_kernel, wq, wv, rank),
        [((seqs * rank, width), bf16), ((seqs, 2, 2 * rank, length), f32)],
        (seq_lengths, got, hidden_in, grad_q, grad_vt),
        scalars=1,
        flops=30_000_000_000,
        name="low_rank",
    )

    low = swap(low.reshape(nx * nc, seqs * 4 * rank // (nx * nc), length), xc)
    low, *far = lax.optimization_barrier((low, *far))
    low = jnp.sum(low, axis=0).astype(bf16)
    low = spread(low, head, nh * nx * nc)
    low = jnp.sum(low.reshape(nh, 4 * seqs, rank, length).astype(f32), axis=0)
    (d_own,) = local(
        functools.partial(adapter_grad_kernel, wq, wv, rank),
        [((nz, seqs * rank, width + 64), bf16)],
        (seq_lengths, task_ids, low, hidden_in, grad_q, grad_vt),
        scalars=2,
        scratch=[pltpu.VMEM((seqs * rank, width + 64), f32)],
        name="adapter_grads",
    )
    d_line = swap(d_own, "zl").reshape(nz * seqs * rank, width + 64)
    d_all = spread(d_line, "y", ny).reshape(batches * rank, width + 64)

    (d_lat,) = local(
        functools.partial(latent_grad_kernel, split, width, rank),
        [((nh * nx * nc, 2 * rows, 128), f32)],
        (d_all, packed),
        name="latent_grads",
    )
    d_lat = swap(d_lat, head)
    g_aq, g_bq, g_av, g_bv, sg_all, embeds = local(
        functools.partial(head_grad_kernel, wq, wv, rank),
        [((rows * rank, wq), f32)] * 3
        + [((rows * rank, wv), f32), ((2 * rows, batches), f32), ((batches, emb), bf16)],
        (d_all, lat_own, sg_own, task_embed),
        name="head_grads",
    )

    blocks = nh * nx
    pair = [(0, 1), (1, 0)]
    base_vt = base_v.T
    part_q = lax.dynamic_index_in_dim(base_q.reshape(blocks, nc, wq, wq), 1 - c, 1, keepdims=False)
    part_vt = lax.dynamic_index_in_dim(base_vt.reshape(wv, blocks, nc, wq), 1 - c, 2, keepdims=False)
    part_q = lax.ppermute(part_q.reshape(blocks * wq, wq), "c", pair)
    part_vt = lax.ppermute(part_vt.reshape(wv, blocks * wq), "c", pair)
    order = []
    for half in range(nh):
        for k in range(nx):
            block = (zh ^ half) * nx + lax.rem(x - k + nx, nx)
            order += [block * nc + c, block]
    acc_q, acc_v, given = local(
        base_kernel,
        [((seqs * length, wq), f32), ((seqs * length, wv), f32), ((seqs * length, wq + wv), bf16)],
        (
            jnp.stack(order).astype(jnp.int32),
            hidden_in,
            *near,
            other,
            *far,
            base_q,
            base_vt,
            part_q,
            part_vt,
        ),
        scalars=1,
        name="base_product",
    )
    q_out, vt_out = local(
        functools.partial(out_kernel, rank),
        [((seqs, length, wq), bf16), ((seqs, wv, length), bf16)],
        (acc_q, acc_v, lax.ppermute(given, "c", pair), low, adapters),
        name="outputs",
    )
    d_lat, sg_all, embeds, g_aq, q_out = lax.optimization_barrier((d_lat, sg_all, embeds, g_aq, q_out))
    g_in, g_mod = local(
        trunk_kernel, [((rows, emb), f32), ((2 * rows, 1), f32)], (d_lat, sg_all, embeds), name="trunk_grads"
    )

    def cube(g):
        return g.reshape(rows, rank, -1)

    return (
        q_out,
        vt_out.swapaxes(1, 2),
        cube(g_aq),
        cube(g_bq),
        cube(g_av),
        cube(g_bv),
        g_in.T,
        g_mod.reshape(2, rows),
    )


def solution(mesh):
    fine = Mesh(mesh.devices.reshape(4, 8, 2, 4, 2), ("y", "zl", "zh", "x", "c"))
    dp, head = ("y", "zl"), ("zh", "x", "c")
    rows_cols = P(dp, None, head)
    return jax.shard_map(
        on_device,
        mesh=fine,
        in_specs=(P(), P(dp), P(dp), P(), P())
        + (rows_cols,) * 4
        + (P(None, head),) * 2
        + (rows_cols,) * 3,
        out_specs=(rows_cols,) * 6 + (P(None, dp),) * 2,
        check_vma=False,
    )
```

```python
import functools

import jax
import jax.numpy as jnp
from jax import lax
from jax.experimental import pallas as pl
from jax.experimental.pallas import tpu as pltpu
from jax.sharding import Mesh, PartitionSpec as P

bf16, f32 = jnp.bfloat16, jnp.float32
exact = lax.Precision.HIGHEST
scale = 2.0


def mm(a, b, dims=((1,), (0,)), precision=None):
    return lax.dot_general(a, b, (dims, ((), ())), precision=precision, preferred_element_type=f32)


def mm_nt(a, b, precision=None):
    return mm(a, b, ((1,), (1,)), precision)


def iota(shape, dim):
    return lax.broadcasted_iota(jnp.int32, shape, dim)


def silu_grad(pre):
    sig = jax.nn.sigmoid(pre)
    return sig * (1.0 + pre * (1.0 - sig))


def swap(blocks, axes):
    return lax.all_to_all(blocks, axes, 0, 0, tiled=True)


def spread(block, axes, n):
    return swap(jnp.broadcast_to(block[None], (n,) + block.shape), axes)


def local(body, outs, args, scalars=0, scratch=(), flops=1_000_000, mib=8, name=None):
    in_vmem = pl.BlockSpec(memory_space=pltpu.VMEM)
    in_smem = pl.BlockSpec(memory_space=pltpu.SMEM)
    return pl.pallas_call(
        body,
        out_shape=tuple(jax.ShapeDtypeStruct(s, d) for s, d in outs),
        in_specs=[in_smem] * scalars + [in_vmem] * (len(args) - scalars),
        out_specs=tuple(in_vmem for _ in outs),
        scratch_shapes=list(scratch),
        compiler_params=pltpu.CompilerParams(vmem_limit_bytes=mib * 2**20),
        cost_estimate=pl.CostEstimate(flops=flops, bytes_accessed=100_000, transcendentals=0),
        name=name,
    )(*args)


def tables_kernel(ny, nz, place, task_embed, w_in, module, lat_line, lat_own, sg_own):
    latents = w_in.shape[1]
    rows = latents // (ny * nz)
    rank = lat_own.shape[2] // rows
    y, z = place[0], place[1]
    pre = mm(task_embed[...], w_in[...])
    q = iota((latents, lat_line.shape[2]), 1)
    line = iota((latents, lat_line.shape[2]), 0) == (
        (q // (rows * rank)) * (nz * rows) + z * rows + (q // rank) % rows
    )
    line = line.astype(f32).astype(bf16)
    first = (y * nz + z) * rows
    q = iota((latents, lat_own.shape[2]), 1)
    own = (iota((latents, lat_own.shape[2]), 0) == first + q // rank).astype(f32).astype(bf16)
    mine = (iota((rows, latents), 1) == first + iota((rows, latents), 0)).astype(f32)
    for m in range(2):
        p = pre + module[m : m + 1, :]
        lat = (p * jax.nn.sigmoid(p)).astype(bf16)
        lat_line[m] = mm(lat, line).astype(bf16)
        lat_own[m] = mm(lat, own).astype(bf16)
        sg_own[m * rows : (m + 1) * rows, :] = mm_nt(mine, silu_grad(p), exact)


def part_kernel(split, rank, ids, lat_line, w_line, part):
    n, k = part.shape[0], w_line.shape[0]
    tasks = lat_line.shape[1]
    at = ids[...].reshape(n, ids.shape[2])[:, :1]
    pick = (iota((n, tasks), 1) == at).astype(f32).astype(bf16)
    same = iota((n, k), 0) % rank == iota((n, k), 1) % rank
    for m, cols in enumerate((slice(0, split), slice(split, None))):
        spread_lat = jnp.where(same, mm(pick, lat_line[m]), 0.0).astype(bf16)
        part[:, cols] = mm(spread_lat, w_line[:, cols]).astype(bf16)


def row_weight(lengths, s, length):
    n = jnp.full((1, length), lengths[s], jnp.int32)
    return jnp.where(iota((1, length), 1) < n, scale / n.astype(f32), 0.0)


def low_kernel(wq, wv, rank, lengths, got, hidden, grad_q, grad_vt, adapters, low):
    total = got[0].astype(f32)
    for i in range(1, got.shape[0]):
        total += got[i].astype(f32)
    adapters[...] = total.astype(bf16)
    total = total.astype(bf16).astype(f32)
    for s in range(hidden.shape[0]):
        own = total[s * rank : (s + 1) * rank, :]
        a = jnp.concatenate([own[:, :wq], own[:, 2 * wq : 3 * wq]], axis=0).astype(bf16)
        b_q, b_v = own[:, wq : 2 * wq].astype(bf16), own[:, 3 * wq :].astype(bf16)
        low[s, 0] = mm_nt(a, hidden[s])
        back = jnp.concatenate([mm_nt(b_q, grad_q[s]), mm(b_v, grad_vt[s])], axis=0)
        low[s, 1] = back * row_weight(lengths, s, hidden.shape[1])


def adapter_grad_kernel(wq, wv, rank, lengths, ids, low, hidden, grad_q, grad_vt, out, rows):
    for s in range(hidden.shape[0]):
        at = slice(s * rank, (s + 1) * rank)
        weight = row_weight(lengths, s, hidden.shape[1])
        du = jnp.concatenate([low[4 * s + 2], low[4 * s + 3]], axis=0).astype(bf16)
        d_a = mm(du, hidden[s])
        rows[at, :wq] = d_a[:rank]
        rows[at, wq : 2 * wq] = mm((low[4 * s] * weight).astype(bf16), grad_q[s])
        rows[at, 2 * wq : 3 * wq] = d_a[rank:]
        rows[at, 3 * wq : 3 * wq + wv] = mm_nt((low[4 * s + 1] * weight).astype(bf16), grad_vt[s])
        rest = rows.shape[1] - 3 * wq - wv
        rows[at, 3 * wq + wv :] = jnp.full((rank, rest), ids[s], jnp.int32).astype(f32)
    done = rows[...].astype(bf16)
    for i in range(out.shape[0]):
        out[i] = done


def latent_grad_kernel(split, width, rank, d_all, weights, out):
    n, k = d_all.shape[0], weights.shape[0]
    same = iota((n, k), 0) % rank == iota((n, k), 1) % rank
    fold = (iota((k // rank, k), 0) == iota((k // rank, k), 1) // rank).astype(f32)
    parts = []
    for cols in (slice(0, split), slice(split, width)):
        full = jnp.where(same, mm_nt(d_all[:, cols], weights[:, cols]), 0.0)
        by_batch = jnp.sum(full.reshape(n // rank, rank, k), axis=1)
        parts.append(mm_nt(fold, by_batch, exact))
    both = jnp.concatenate(parts, axis=1)
    for i in range(out.shape[0]):
        out[i] = both


def head_grad_kernel(wq, wv, rank, d_all, lat_own, sg_own, task_embed, g_aq, g_bq, g_av, g_bv, sg_all, embeds):
    n, k = d_all.shape[0], lat_own.shape[2]
    tasks = lat_own.shape[1]
    width = 3 * wq + wv
    tail = d_all[:, 3 * wq :].astype(f32)
    pick = (iota((n, tasks), 1).astype(f32) == tail[:, wv : wv + 1]).astype(f32)
    same = iota((n, k), 0) % rank == iota((n, k), 1) % rank
    lat = [jnp.where(same, mm(pick.astype(bf16), lat_own[m]), 0.0).astype(bf16) for m in range(2)]
    g_q = mm(lat[0], d_all[:, : 2 * wq], ((0,), (0,)))
    g_aq[...], g_bq[...] = g_q[:, :wq], g_q[:, wq:]
    g_v = mm(lat[1], d_all[:, 2 * wq : width], ((0,), (0,)))
    g_av[...], g_bv[...] = g_v[:, :wq], g_v[:, wq:]
    one = jnp.where(iota((n, tasks), 0) % rank == 0, pick, 0.0)
    one = jnp.sum(one.reshape(n // rank, rank, tasks), axis=1)
    sg_all[...] = mm_nt(sg_own[...], one, exact)
    embeds[...] = mm(one.astype(bf16), task_embed[...]).astype(bf16)


def trunk_kernel(got, sg_all, embeds, g_in, g_mod):
    total = got[0]
    for i in range(1, got.shape[0]):
        total += got[i]
    rows, batches = sg_all.shape
    total = jnp.concatenate([total[:, :batches], total[:, batches:]], axis=0)
    d_pre = total * sg_all[...]
    both = d_pre[: rows // 2] + d_pre[rows // 2 :]
    hi = both.astype(bf16)
    lo = (both - hi.astype(f32)).astype(bf16)
    g_in[...] = mm(hi, embeds[...]) + mm(lo, embeds[...])
    g_mod[...] = jnp.sum(d_pre, axis=1, keepdims=True)


def give_kernel(core, base_q, base_vt, out):
    wq, wv = base_q.shape[1], base_vt.shape[0]
    out[...] = jnp.zeros_like(out)
    for n in range(out.shape[0] // wq):
        at = pl.ds(pl.multiple_of((2 * n + core[0]) * wq, wq), wq)
        to = slice(n * wq, (n + 1) * wq)
        out[to, :wq] = base_q[at, :]
        out[to, wq : wq + wv] = base_vt[:, at].astype(f32).T.astype(bf16)


def base_kernel(order, *refs):
    near = refs[:4]
    base_q, base_vt, theirs, acc_q, acc_v, out = refs[4:]
    halves, seqs, length, wq = near[0].shape
    for n in range(halves * len(near)):
        h = near[n // halves][n % halves].reshape(seqs * length, wq)
        at = pl.ds(pl.multiple_of(order[2 * n] * wq, wq), wq)
        far = pl.ds(pl.multiple_of(order[2 * n + 1] * wq, wq), wq)
        adds = mm(h, base_q[at, :]), mm_nt(h, base_vt[:, at])
        partner = mm(h, theirs[far, :])
        if n == 0:
            acc_q[...], acc_v[...] = adds
            both = partner
        else:
            acc_q[...] += adds[0]
            acc_v[...] += adds[1]
            both += partner
    out[...] = both[:, : out.shape[1]].astype(bf16)


def out_kernel(rank, core, acc_q, acc_v, got, low, ad, q_out, vt_out):
    seqs, length, wq = q_out.shape
    both = ad[...].astype(f32)
    first = ((0,), (0,))
    for s in range(seqs):
        own = slice(s * length, (s + 1) * length)
        b = both[s * rank : (s + 1) * rank, :].astype(bf16)
        low_q = mm(low[4 * s].astype(bf16), b[:, wq : 2 * wq], first)
        low_v = mm(b[:, 3 * wq :], low[4 * s + 1].astype(bf16), first)
        theirs = got[core[0], own, :].astype(f32)
        got_q, got_v = theirs[:, :wq], theirs[:, wq:]
        q_out[s] = (acc_q[own, :] + got_q + scale * low_q).astype(bf16)
        vt_out[s] = ((acc_v[own, :] + got_v).T + scale * low_v).astype(bf16)


def on_device(
    task_embed,
    task_ids,
    seq_lengths,
    w_in,
    module_embed,
    wa_q,
    wb_q,
    wa_v,
    wb_v,
    base_q,
    base_v,
    hidden_in,
    grad_q,
    grad_v,
):
    ny, nz, nh, nx, nc = (lax.axis_size(a) for a in ("y", "zl", "zh", "x", "c"))
    y, zl, zh, x, c = (lax.axis_index(a) for a in ("y", "zl", "zh", "x", "c"))
    xc, head = ("x", "c"), ("zh", "x", "c")
    seqs, length, wq = hidden_in.shape
    rows, rank, _ = wa_q.shape
    wv = wb_v.shape[2]
    tasks, emb = task_embed.shape
    split, width = 2 * wq, 3 * wq + wv
    batches = seqs * ny * nz
    grad_vt = grad_v.swapaxes(1, 2)

    packed = jnp.concatenate([wa_q, wb_q, wa_v, wb_v], axis=2).reshape(rows * rank, width)
    w_line = lax.all_gather(packed, "y", axis=0, tiled=True)
    ids, w_line = lax.optimization_barrier((task_ids, w_line))
    ids_rows = jnp.broadcast_to(ids[:, None, None], (seqs, rank, 128)).reshape(seqs * rank, 128)
    ids_line = spread(ids_rows, "zl", nz)
    lat_line, lat_own, sg_own = local(
        functools.partial(tables_kernel, ny, nz),
        [((2, tasks, ny * rows * rank), bf16), ((2, tasks, rows * rank), bf16), ((2 * rows, tasks), f32)],
        (jnp.stack([y, zl]).astype(jnp.int32), task_embed, w_in, module_embed),
        scalars=1,
        name="tables",
    )
    other = lax.ppermute(hidden_in, "zh", [(0, 1), (1, 0)])
    ids_line, w_line, other = lax.optimization_barrier((ids_line, w_line, other))

    (part,) = local(
        functools.partial(part_kernel, split, rank),
        [((nz * seqs * rank, width), bf16)],
        (ids_line, lat_line, w_line),
        name="adapter_parts",
    )
    got = swap(part.reshape(nz, seqs * rank, width), "zl")
    adapters, low = local(
        functools.partial(low_kernel, wq, wv, rank),
        [((seqs * rank, width), bf16), ((seqs, 2, 2 * rank, length), f32)],
        (seq_lengths, got, hidden_in, grad_q, grad_vt),
        scalars=1,
        name="low_rank",
    )

    low = swap(low.reshape(nx * nc, seqs * 4 * rank // (nx * nc), length), xc)
    low = jnp.sum(low, axis=0).astype(bf16)
    low = spread(low, head, nh * nx * nc)

    blocks = nh * nx
    pair = [(0, 1), (1, 0)]
    base_vt = base_v.T
    (theirs,) = local(
        give_kernel,
        [((blocks * wq, wq + 128), bf16)],
        (jnp.reshape(1 - c, (1,)).astype(jnp.int32), base_q, base_vt),
        scalars=1,
        name="partner_rows",
    )
    theirs = lax.ppermute(theirs, "c", pair)
    low = jnp.sum(low.reshape(nh, 4 * seqs, rank, length).astype(f32), axis=0)
    (d_own,) = local(
        functools.partial(adapter_grad_kernel, wq, wv, rank),
        [((nz, seqs * rank, width + 64), bf16)],
        (seq_lengths, task_ids, low, hidden_in, grad_q, grad_vt),
        scalars=2,
        scratch=[pltpu.VMEM((seqs * rank, width + 64), f32)],
        name="adapter_grads",
    )
    d_line = swap(d_own, "zl").reshape(nz * seqs * rank, width + 64)
    d_all = lax.all_gather(d_line, "y", axis=0, tiled=True)

    both_z = jnp.stack([hidden_in, other])
    turned = [both_z] + [lax.ppermute(both_z, "x", [(i, (i + k) % nx) for i in range(nx)]) for k in range(1, nx)]
    order = []
    for k in range(nx):
        for half in range(nh):
            block = (zh ^ half) * nx + lax.rem(x - k + nx, nx)
            order += [block * nc + c, block]
    order = jnp.stack(order).astype(jnp.int32)
    d_all, order = lax.optimization_barrier((d_all, order))
    acc_q, acc_v, given = local(
        base_kernel,
        [((seqs * length, wq), f32), ((seqs * length, wv), f32), ((seqs * length, wq + wv), bf16)],
        (
            order,
            *turned,
            base_q,
            base_vt,
            theirs,
        ),
        scalars=1,
        mib=20,
        name="base_product",
    )
    (d_lat,) = local(
        functools.partial(latent_grad_kernel, split, width, rank),
        [((nh * nx * nc, rows, 2 * batches), f32)],
        (d_all, packed),
        name="latent_grads",
    )
    d_lat = swap(d_lat, head)
    g_aq, g_bq, g_av, g_bv, sg_all, embeds = local(
        functools.partial(head_grad_kernel, wq, wv, rank),
        [((rows * rank, wq), f32)] * 3
        + [((rows * rank, wv), f32), ((2 * rows, batches), f32), ((batches, emb), bf16)],
        (d_all, lat_own, sg_own, task_embed),
        name="head_grads",
    )

    q_out, vt_out = local(
        functools.partial(out_kernel, rank),
        [((seqs, length, wq), bf16), ((seqs, wv, length), bf16)],
        (jnp.reshape(1 - c, (1,)).astype(jnp.int32), acc_q, acc_v, lax.all_gather(given, "c"), low, adapters),
        scalars=1,
        name="outputs",
    )
    d_lat, sg_all, embeds, g_aq, q_out = lax.optimization_barrier((d_lat, sg_all, embeds, g_aq, q_out))
    g_in, g_mod = local(
        trunk_kernel, [((rows, emb), f32), ((2 * rows, 1), f32)], (d_lat, sg_all, embeds), name="trunk_grads"
    )

    def cube(g):
        return g.reshape(rows, rank, -1)

    return (
        q_out,
        vt_out.swapaxes(1, 2),
        cube(g_aq),
        cube(g_bq),
        cube(g_av),
        cube(g_bv),
        g_in.T,
        g_mod.reshape(2, rows),
    )


def solution(mesh):
    fine = Mesh(mesh.devices.reshape(4, 8, 2, 4, 2), ("y", "zl", "zh", "x", "c"))
    dp, head = ("y", "zl"), ("zh", "x", "c")
    rows_cols = P(dp, None, head)
    return jax.shard_map(
        on_device,
        mesh=fine,
        in_specs=(P(), P(dp), P(dp), P(), P())
        + (rows_cols,) * 4
        + (P(None, head),) * 2
        + (rows_cols,) * 3,
        out_specs=(rows_cols,) * 6 + (P(None, dp),) * 2,
        check_vma=False,
    )
```

```python
import functools

import jax
import jax.numpy as jnp
from jax import lax
from jax.experimental import pallas as pl
from jax.experimental.pallas import tpu as pltpu
from jax.sharding import Mesh, PartitionSpec as P

bf16, f32 = jnp.bfloat16, jnp.float32
exact = lax.Precision.HIGHEST
scale = 2.0


def mm(a, b, dims=((1,), (0,)), precision=None):
    return lax.dot_general(a, b, (dims, ((), ())), precision=precision, preferred_element_type=f32)


def mm_nt(a, b, precision=None):
    return mm(a, b, ((1,), (1,)), precision)


def iota(shape, dim):
    return lax.broadcasted_iota(jnp.int32, shape, dim)


def silu_grad(pre):
    sig = jax.nn.sigmoid(pre)
    return sig * (1.0 + pre * (1.0 - sig))


def swap(blocks, axes):
    return lax.all_to_all(blocks, axes, 0, 0, tiled=True)


def spread(block, axes, n):
    return swap(jnp.broadcast_to(block[None], (n,) + block.shape), axes)


def local(body, outs, args, scalars=0, scratch=(), flops=1_000_000, mib=8, name=None):
    in_vmem = pl.BlockSpec(memory_space=pltpu.VMEM)
    in_smem = pl.BlockSpec(memory_space=pltpu.SMEM)
    return pl.pallas_call(
        body,
        out_shape=tuple(jax.ShapeDtypeStruct(s, d) for s, d in outs),
        in_specs=[in_smem] * scalars + [in_vmem] * (len(args) - scalars),
        out_specs=tuple(in_vmem for _ in outs),
        scratch_shapes=list(scratch),
        compiler_params=pltpu.CompilerParams(vmem_limit_bytes=mib * 2**20),
        cost_estimate=pl.CostEstimate(flops=flops, bytes_accessed=100_000, transcendentals=0),
        name=name,
    )(*args)


def tables_kernel(task_embed, w_in, module, lat_line, lat_own, sg_own):
    ny, nz = lax.axis_size("y"), lax.axis_size("zl")
    latents = w_in.shape[1]
    rows = latents // (ny * nz)
    rank = lat_own.shape[2] // rows
    y, z = lax.axis_index("y"), lax.axis_index("zl")
    pre = mm(task_embed[...], w_in[...])
    q = iota((latents, lat_line.shape[2]), 1)
    line = iota((latents, lat_line.shape[2]), 0) == (
        (q // (rows * rank)) * (nz * rows) + z * rows + (q // rank) % rows
    )
    line = line.astype(f32).astype(bf16)
    first = (y * nz + z) * rows
    q = iota((latents, lat_own.shape[2]), 1)
    own = (iota((latents, lat_own.shape[2]), 0) == first + q // rank).astype(f32).astype(bf16)
    mine = (iota((rows, latents), 1) == first + iota((rows, latents), 0)).astype(f32)
    for m in range(2):
        p = pre + module[m : m + 1, :]
        lat = (p * jax.nn.sigmoid(p)).astype(bf16)
        lat_line[m] = mm(lat, line).astype(bf16)
        lat_own[m] = mm(lat, own).astype(bf16)
        sg_own[m * rows : (m + 1) * rows, :] = mm_nt(mine, silu_grad(p), exact)


def part_kernel(split, rank, ids, lat_line, w_line, part):
    n, k = part.shape[0], w_line.shape[0]
    tasks = lat_line.shape[1]
    at = ids[...].reshape(n, ids.shape[2])[:, :1]
    pick = (iota((n, tasks), 1) == at).astype(f32).astype(bf16)
    same = iota((n, k), 0) % rank == iota((n, k), 1) % rank
    for m, cols in enumerate((slice(0, split), slice(split, None))):
        spread_lat = jnp.where(same, mm(pick, lat_line[m]), 0.0).astype(bf16)
        part[:, cols] = mm(spread_lat, w_line[:, cols]).astype(bf16)


def row_weight(lengths, s, length):
    n = jnp.full((1, length), lengths[s], jnp.int32)
    return jnp.where(iota((1, length), 1) < n, scale / n.astype(f32), 0.0)


def low_kernel(wq, wv, rank, lengths, got, hidden, grad_q, grad_vt, adapters, low):
    total = got[0].astype(f32)
    for i in range(1, got.shape[0]):
        total += got[i].astype(f32)
    adapters[...] = total.astype(bf16)
    total = total.astype(bf16).astype(f32)
    for s in range(hidden.shape[0]):
        own = total[s * rank : (s + 1) * rank, :]
        a = jnp.concatenate([own[:, :wq], own[:, 2 * wq : 3 * wq]], axis=0).astype(bf16)
        b_q, b_v = own[:, wq : 2 * wq].astype(bf16), own[:, 3 * wq :].astype(bf16)
        low[s, 0] = mm_nt(a, hidden[s])
        back = jnp.concatenate([mm_nt(b_q, grad_q[s]), mm(b_v, grad_vt[s])], axis=0)
        low[s, 1] = back * row_weight(lengths, s, hidden.shape[1])


def sum_halves(low, rank):
    both = low[...].astype(f32)
    rows = both.shape[0] // 2
    return (both[:rows] + both[rows:]).reshape(rows // rank, rank, both.shape[1])


def adapter_grad_kernel(wq, wv, rank, lengths, ids, low, hidden, grad_q, grad_vt, out, rows):
    low = sum_halves(low, rank)
    for s in range(hidden.shape[0]):
        at = slice(s * rank, (s + 1) * rank)
        weight = row_weight(lengths, s, hidden.shape[1])
        du = jnp.concatenate([low[4 * s + 2], low[4 * s + 3]], axis=0).astype(bf16)
        d_a = mm(du, hidden[s])
        rows[at, :wq] = d_a[:rank]
        rows[at, wq : 2 * wq] = mm((low[4 * s] * weight).astype(bf16), grad_q[s])
        rows[at, 2 * wq : 3 * wq] = d_a[rank:]
        rows[at, 3 * wq : 3 * wq + wv] = mm_nt((low[4 * s + 1] * weight).astype(bf16), grad_vt[s])
        rest = rows.shape[1] - 3 * wq - wv
        rows[at, 3 * wq + wv :] = jnp.full((rank, rest), ids[s], jnp.int32).astype(f32)
    done = rows[...].astype(bf16)
    for i in range(out.shape[0]):
        out[i] = done


def latent_grad_kernel(split, width, rank, d_all, weights, out):
    n, k = d_all.shape[0], weights.shape[0]
    same = iota((n, k), 0) % rank == iota((n, k), 1) % rank
    fold = (iota((k // rank, k), 0) == iota((k // rank, k), 1) // rank).astype(f32)
    parts = []
    for cols in (slice(0, split), slice(split, width)):
        full = jnp.where(same, mm_nt(d_all[:, cols], weights[:, cols]), 0.0)
        by_batch = jnp.sum(full.reshape(n // rank, rank, k), axis=1)
        parts.append(mm_nt(fold, by_batch, exact))
    both = jnp.concatenate(parts, axis=1)
    for i in range(out.shape[0]):
        out[i] = both


def head_grad_kernel(wq, wv, rank, d_all, lat_own, sg_own, task_embed, g_aq, g_bq, g_av, g_bv, sg_all, embeds):
    n, k = d_all.shape[0], lat_own.shape[2]
    tasks = lat_own.shape[1]
    width = 3 * wq + wv
    tail = d_all[:, 3 * wq :].astype(f32)
    pick = (iota((n, tasks), 1).astype(f32) == tail[:, wv : wv + 1]).astype(f32)
    same = iota((n, k), 0) % rank == iota((n, k), 1) % rank
    lat = [jnp.where(same, mm(pick.astype(bf16), lat_own[m]), 0.0).astype(bf16) for m in range(2)]
    g_q = mm(lat[0], d_all[:, : 2 * wq], ((0,), (0,)))
    g_aq[...], g_bq[...] = g_q[:, :wq], g_q[:, wq:]
    g_v = mm(lat[1], d_all[:, 2 * wq : width], ((0,), (0,)))
    g_av[...], g_bv[...] = g_v[:, :wq], g_v[:, wq:]
    one = jnp.where(iota((n, tasks), 0) % rank == 0, pick, 0.0)
    one = jnp.sum(one.reshape(n // rank, rank, tasks), axis=1)
    sg_all[...] = mm_nt(sg_own[...], one, exact)
    embeds[...] = mm(one.astype(bf16), task_embed[...]).astype(bf16)


def trunk_kernel(got, sg_all, embeds, g_in, g_mod):
    total = got[0]
    for i in range(1, got.shape[0]):
        total += got[i]
    rows, batches = sg_all.shape
    total = jnp.concatenate([total[:, :batches], total[:, batches:]], axis=0)
    d_pre = total * sg_all[...]
    both = d_pre[: rows // 2] + d_pre[rows // 2 :]
    hi = both.astype(bf16)
    lo = (both - hi.astype(f32)).astype(bf16)
    g_in[...] = mm(hi, embeds[...]) + mm(lo, embeds[...])
    ones = jnp.ones((1, batches), f32)
    for m in range(2):
        g_mod[m : m + 1, :] = mm_nt(ones, d_pre[m * rows // 2 : (m + 1) * rows // 2], exact)


def give_kernel(base_q, base_vt, out):
    partner = 1 - lax.axis_index("c")
    wq, wv = base_q.shape[1], base_vt.shape[0]
    out[...] = jnp.zeros_like(out)
    for n in range(out.shape[0] // wq):
        at = pl.ds(pl.multiple_of((2 * n + partner) * wq, wq), wq)
        to = slice(n * wq, (n + 1) * wq)
        out[to, :wq] = base_q[at, :]
        out[to, wq : wq + wv] = base_vt[:, at].astype(f32).T.astype(bf16)


def base_kernel(*refs):
    near = refs[:4]
    base_q, base_vt, theirs, acc_q, acc_v, out = refs[4:]
    halves, seqs, length, wq = near[0].shape
    zh, x, c = (lax.axis_index(a) for a in ("zh", "x", "c"))
    nx, nc = len(near), lax.axis_size("c")
    for n in range(halves * nx):
        k, half = n // halves, n % halves
        block = lax.rem(zh + half, halves) * nx + lax.rem(x - k + nx, nx)
        h = near[n // halves][n % halves].reshape(seqs * length, wq)
        at = pl.ds(pl.multiple_of((block * nc + c) * wq, wq), wq)
        far = pl.ds(pl.multiple_of(block * wq, wq), wq)
        adds = mm(h, base_q[at, :]), mm_nt(h, base_vt[:, at])
        partner = mm(h, theirs[far, :])
        if n == 0:
            acc_q[...], acc_v[...] = adds
            both = partner
        else:
            acc_q[...] += adds[0]
            acc_v[...] += adds[1]
            both += partner
    out[...] = both[:, : out.shape[1]].astype(bf16)


def out_kernel(rank, acc_q, acc_v, got, low, ad, q_out, vt_out):
    low = sum_halves(low, rank)
    partner = 1 - lax.axis_index("c")
    seqs, length, wq = q_out.shape
    both = ad[...].astype(f32)
    first = ((0,), (0,))
    for s in range(seqs):
        own = slice(s * length, (s + 1) * length)
        b = both[s * rank : (s + 1) * rank, :].astype(bf16)
        low_q = mm(low[4 * s].astype(bf16), b[:, wq : 2 * wq], first)
        low_v = mm(b[:, 3 * wq :], low[4 * s + 1].astype(bf16), first)
        theirs = got[partner, own, :].astype(f32)
        got_q, got_v = theirs[:, :wq], theirs[:, wq:]
        q_out[s] = (acc_q[own, :] + got_q + scale * low_q).astype(bf16)
        vt_out[s] = ((acc_v[own, :] + got_v).T + scale * low_v).astype(bf16)


def on_device(
    task_embed,
    task_ids,
    seq_lengths,
    w_in,
    module_embed,
    wa_q,
    wb_q,
    wa_v,
    wb_v,
    base_q,
    base_v,
    hidden_in,
    grad_q,
    grad_v,
):
    ny, nz, nh, nx, nc = (lax.axis_size(a) for a in ("y", "zl", "zh", "x", "c"))
    xc, head = ("x", "c"), ("zh", "x", "c")
    seqs, length, wq = hidden_in.shape
    rows, rank, _ = wa_q.shape
    wv = wb_v.shape[2]
    tasks, emb = task_embed.shape
    split, width = 2 * wq, 3 * wq + wv
    batches = seqs * ny * nz
    grad_vt = grad_v.swapaxes(1, 2)

    packed = jnp.concatenate([wa_q, wb_q, wa_v, wb_v], axis=2).reshape(rows * rank, width)
    w_line = lax.all_gather(packed, "y", axis=0, tiled=True)
    ids_rows = jnp.broadcast_to(task_ids[None, :, None, None], (nz, seqs, rank, 128))
    ids_rows, w_line = lax.optimization_barrier((ids_rows.reshape(nz, seqs * rank, 128), w_line))
    ids_line = swap(ids_rows, "zl")
    lat_line, lat_own, sg_own = local(
        tables_kernel,
        [((2, tasks, ny * rows * rank), bf16), ((2, tasks, rows * rank), bf16), ((2 * rows, tasks), f32)],
        (task_embed, w_in, module_embed),
        name="tables",
    )
    other = lax.ppermute(hidden_in, "zh", [(0, 1), (1, 0)])
    ids_line, w_line, other = lax.optimization_barrier((ids_line, w_line, other))

    (part,) = local(
        functools.partial(part_kernel, split, rank),
        [((nz * seqs * rank, width), bf16)],
        (ids_line, lat_line, w_line),
        name="adapter_parts",
    )
    got = swap(part.reshape(nz, seqs * rank, width), "zl")
    adapters, low = local(
        functools.partial(low_kernel, wq, wv, rank),
        [((seqs * rank, width), bf16), ((seqs, 2, 2 * rank, length), f32)],
        (seq_lengths, got, hidden_in, grad_q, grad_vt),
        scalars=1,
        name="low_rank",
    )

    low = swap(low.reshape(nx * nc, seqs * 4 * rank // (nx * nc), length), xc)
    low = jnp.sum(low, axis=0).astype(bf16)
    low = spread(low, head, nh * nx * nc)

    blocks = nh * nx
    pair = [(0, 1), (1, 0)]
    base_vt = base_v.T
    (theirs,) = local(
        give_kernel,
        [((blocks * wq, wq + 128), bf16)],
        (base_q, base_vt),
        name="partner_rows",
    )
    theirs = lax.ppermute(theirs, "c", pair)
    low = low.reshape(nh * 4 * seqs * rank, length)
    (d_own,) = local(
        functools.partial(adapter_grad_kernel, wq, wv, rank),
        [((nz, seqs * rank, width + 64), bf16)],
        (seq_lengths, task_ids, low, hidden_in, grad_q, grad_vt),
        scalars=2,
        scratch=[pltpu.VMEM((seqs * rank, width + 64), f32)],
        name="adapter_grads",
    )
    d_line = swap(d_own, "zl").reshape(nz * seqs * rank, width + 64)
    d_all = lax.all_gather(d_line, "y", axis=0, tiled=True)

    both_z = jnp.stack([hidden_in, other])
    turned = [both_z] + [lax.ppermute(both_z, "x", [(i, (i + k) % nx) for i in range(nx)]) for k in range(1, nx)]
    d_all, theirs = lax.optimization_barrier((d_all, theirs))
    acc_q, acc_v, given = local(
        base_kernel,
        [((seqs * length, wq), f32), ((seqs * length, wv), f32), ((seqs * length, wq + wv), bf16)],
        (
            *turned,
            base_q,
            base_vt,
            theirs,
        ),
        mib=20,
        name="base_product",
    )
    (d_lat,) = local(
        functools.partial(latent_grad_kernel, split, width, rank),
        [((nh * nx * nc, rows, 2 * batches), f32)],
        (d_all, packed),
        name="latent_grads",
    )
    d_lat = swap(d_lat, head)
    g_aq, g_bq, g_av, g_bv, sg_all, embeds = local(
        functools.partial(head_grad_kernel, wq, wv, rank),
        [((rows * rank, wq), f32)] * 3
        + [((rows * rank, wv), f32), ((2 * rows, batches), f32), ((batches, emb), bf16)],
        (d_all, lat_own, sg_own, task_embed),
        name="head_grads",
    )

    q_out, vt_out = local(
        functools.partial(out_kernel, rank),
        [((seqs, length, wq), bf16), ((seqs, wv, length), bf16)],
        (acc_q, acc_v, lax.all_gather(given, "c"), low, adapters),
        name="outputs",
    )
    d_lat, g_aq, q_out = lax.optimization_barrier((d_lat, g_aq, q_out))
    g_in, g_mod = local(
        trunk_kernel, [((rows, emb), f32), ((2, rows), f32)], (d_lat, sg_all, embeds), name="trunk_grads"
    )

    def cube(g):
        return g.reshape(rows, rank, -1)

    return (
        q_out,
        vt_out.swapaxes(1, 2),
        cube(g_aq),
        cube(g_bq),
        cube(g_av),
        cube(g_bv),
        g_in.T,
        g_mod,
    )


def solution(mesh):
    fine = Mesh(mesh.devices.reshape(4, 8, 2, 4, 2), ("y", "zl", "zh", "x", "c"))
    dp, head = ("y", "zl"), ("zh", "x", "c")
    rows_cols = P(dp, None, head)
    return jax.shard_map(
        on_device,
        mesh=fine,
        in_specs=(P(), P(dp), P(dp), P(), P())
        + (rows_cols,) * 4
        + (P(None, head),) * 2
        + (rows_cols,) * 3,
        out_specs=(rows_cols,) * 6 + (P(None, dp),) * 2,
        check_vma=False,
    )
```

```python
import functools

import jax
import jax.numpy as jnp
from jax import lax
from jax.experimental import pallas as pl
from jax.experimental.pallas import tpu as pltpu
from jax.sharding import Mesh, PartitionSpec as P

bf16, f32 = jnp.bfloat16, jnp.float32
exact = lax.Precision.HIGHEST
scale = 2.0


def mm(a, b, dims=((1,), (0,)), precision=None):
    return lax.dot_general(a, b, (dims, ((), ())), precision=precision, preferred_element_type=f32)


def mm_nt(a, b, precision=None):
    return mm(a, b, ((1,), (1,)), precision)


def iota(shape, dim):
    return lax.broadcasted_iota(jnp.int32, shape, dim)


def silu_grad(pre):
    sig = jax.nn.sigmoid(pre)
    return sig * (1.0 + pre * (1.0 - sig))


def swap(blocks, axes):
    return lax.all_to_all(blocks, axes, 0, 0, tiled=True)


def spread(block, axes, n):
    return swap(jnp.broadcast_to(block[None], (n,) + block.shape), axes)


def local(body, outs, args, scalars=0, scratch=(), flops=1_000_000, mib=8, name=None):
    in_vmem = pl.BlockSpec(memory_space=pltpu.VMEM)
    in_smem = pl.BlockSpec(memory_space=pltpu.SMEM)
    return pl.pallas_call(
        body,
        out_shape=tuple(jax.ShapeDtypeStruct(s, d) for s, d in outs),
        in_specs=[in_smem] * scalars + [in_vmem] * (len(args) - scalars),
        out_specs=tuple(in_vmem for _ in outs),
        scratch_shapes=list(scratch),
        compiler_params=pltpu.CompilerParams(vmem_limit_bytes=mib * 2**20),
        cost_estimate=pl.CostEstimate(flops=flops, bytes_accessed=100_000, transcendentals=0),
        name=name,
    )(*args)


def tables_kernel(task_embed, w_in, module, lat_line, lat_own, sg_own):
    ny, nz = lax.axis_size("y"), lax.axis_size("zl")
    latents = w_in.shape[1]
    rows = latents // (ny * nz)
    rank = lat_own.shape[2] // rows
    y, z = lax.axis_index("y"), lax.axis_index("zl")
    pre = mm(task_embed[...], w_in[...])
    q = iota((latents, lat_line.shape[2]), 1)
    line = iota((latents, lat_line.shape[2]), 0) == (
        (q // (rows * rank)) * (nz * rows) + z * rows + (q // rank) % rows
    )
    line = line.astype(f32).astype(bf16)
    first = (y * nz + z) * rows
    q = iota((latents, lat_own.shape[2]), 1)
    own = (iota((latents, lat_own.shape[2]), 0) == first + q // rank).astype(f32).astype(bf16)
    mine = (iota((rows, latents), 1) == first + iota((rows, latents), 0)).astype(f32)
    for m in range(2):
        p = pre + module[m : m + 1, :]
        lat = (p * jax.nn.sigmoid(p)).astype(bf16)
        lat_line[m] = mm(lat, line).astype(bf16)
        lat_own[m] = mm(lat, own).astype(bf16)
        sg_own[m * rows : (m + 1) * rows, :] = mm_nt(mine, silu_grad(p), exact)


def pick_tasks(ids, tasks):
    at = ids[...].reshape(ids.shape[0] * ids.shape[1], ids.shape[2])[:, :1]
    return (iota((at.shape[0], tasks), 1) == at).astype(f32).astype(bf16)


def batch_kernel(rank, ids, lat_own, sg_own, task_embed, lat_rows, sg_all, embeds):
    of_all = pick_tasks(ids, lat_own.shape[1])
    ny, nz = lax.axis_size("y"), lax.axis_size("zl")
    batches = of_all.shape[0]
    seqs = batches // (ny * nz)

    def ordered(repeat):
        i, j = iota((batches * repeat, batches), 0) // repeat, iota((batches * repeat, batches), 1)
        hit = (i // (nz * seqs) == (j // seqs) % ny) & ((i // seqs) % nz == j // (seqs * ny)) & (i % seqs == j % seqs)
        return mm(hit.astype(f32).astype(bf16), of_all)

    n, k = lat_rows.shape[1:]
    pick = ordered(rank).astype(bf16)
    same = iota((n, k), 0) % rank == iota((n, k), 1) % rank
    for m in range(2):
        lat_rows[m] = jnp.where(same, mm(pick, lat_own[m]), 0.0).astype(bf16)
    one = ordered(1)
    sg_all[...] = mm_nt(sg_own[...], one, exact)
    embeds[...] = mm(one.astype(bf16), task_embed[...]).astype(bf16)


def part_kernel(split, rank, ids, lat_line, w_line, part):
    n, k = part.shape[0], w_line.shape[0]
    of_all = pick_tasks(ids, lat_line.shape[1])
    i, j = iota((n, of_all.shape[0]), 0), iota((n, of_all.shape[0]), 1)
    ny, y = lax.axis_size("y"), lax.axis_index("y")
    seqs = ids.shape[1] // ny
    mine = (i // (seqs * rank) == j // (seqs * ny)) & ((i // rank) % seqs == j % seqs) & ((j // seqs) % ny == y)
    pick = mm(mine.astype(f32).astype(bf16), of_all).astype(bf16)
    same = iota((n, k), 0) % rank == iota((n, k), 1) % rank
    for m, cols in enumerate((slice(0, split), slice(split, part.shape[1]))):
        spread_lat = jnp.where(same, mm(pick, lat_line[m]), 0.0).astype(bf16)
        part[:, cols] = mm(spread_lat, w_line[:, cols]).astype(bf16)


def row_weight(lengths, s, length):
    n = jnp.full((1, length), lengths[s], jnp.int32)
    return jnp.where(iota((1, length), 1) < n, scale / n.astype(f32), 0.0)


def low_kernel(wq, wv, rank, lengths, got, hidden, grad_q, grad_vt, adapters, low):
    total = got[0].astype(f32)
    for i in range(1, got.shape[0]):
        total += got[i].astype(f32)
    adapters[...] = total.astype(bf16)
    total = total.astype(bf16).astype(f32)
    for s in range(hidden.shape[0]):
        own = total[s * rank : (s + 1) * rank, :]
        a = jnp.concatenate([own[:, :wq], own[:, 2 * wq : 3 * wq]], axis=0).astype(bf16)
        b_q, b_v = own[:, wq : 2 * wq].astype(bf16), own[:, 3 * wq :].astype(bf16)
        low[s, 0] = mm_nt(a, hidden[s])
        back = jnp.concatenate([mm_nt(b_q, grad_q[s]), mm(b_v, grad_vt[s])], axis=0)
        low[s, 1] = back * row_weight(lengths, s, hidden.shape[1])


def sum_halves(low, rank):
    both = low[...].astype(f32)
    rows = both.shape[0] // 2
    return (both[:rows] + both[rows:]).reshape(rows // rank, rank, both.shape[1])


def adapter_grad_kernel(wq, wv, rank, lengths, ids, low, hidden, grad_q, grad_vt, out, rows):
    low = sum_halves(low, rank)
    for s in range(hidden.shape[0]):
        at = slice(s * rank, (s + 1) * rank)
        weight = row_weight(lengths, s, hidden.shape[1])
        du = jnp.concatenate([low[4 * s + 2], low[4 * s + 3]], axis=0).astype(bf16)
        d_a = mm(du, hidden[s])
        rows[at, :wq] = d_a[:rank]
        rows[at, wq : 2 * wq] = mm((low[4 * s] * weight).astype(bf16), grad_q[s])
        rows[at, 2 * wq : 3 * wq] = d_a[rank:]
        rows[at, 3 * wq : 3 * wq + wv] = mm_nt((low[4 * s + 1] * weight).astype(bf16), grad_vt[s])
        rest = rows.shape[1] - 3 * wq - wv
        rows[at, 3 * wq + wv :] = jnp.full((rank, rest), ids[s], jnp.int32).astype(f32)
    done = rows[...].astype(bf16)
    for i in range(out.shape[0]):
        out[i] = done


def latent_grad_kernel(split, width, rank, d_all, weights, out):
    n, k = d_all.shape[0], weights.shape[0]
    same = iota((n, k), 0) % rank == iota((n, k), 1) % rank
    fold = (iota((k // rank, k), 0) == iota((k // rank, k), 1) // rank).astype(f32)
    parts = []
    for cols in (slice(0, split), slice(split, width)):
        full = jnp.where(same, mm_nt(d_all[:, cols], weights[:, cols]), 0.0)
        by_batch = jnp.sum(full.reshape(n // rank, rank, k), axis=1)
        parts.append(mm_nt(fold, by_batch, exact))
    both = jnp.concatenate(parts, axis=1)
    for i in range(out.shape[0]):
        out[i] = both


def head_grad_kernel(wq, wv, d_all, lat_rows, g_aq, g_bq, g_av, g_bv):
    width = 3 * wq + wv
    g_q = mm(lat_rows[0], d_all[:, : 2 * wq], ((0,), (0,)))
    g_aq[...], g_bq[...] = g_q[:, :wq], g_q[:, wq:]
    g_v = mm(lat_rows[1], d_all[:, 2 * wq : width], ((0,), (0,)))
    g_av[...], g_bv[...] = g_v[:, :wq], g_v[:, wq:]


def trunk_kernel(got, sg_all, embeds, g_in, g_mod):
    total = got[0]
    for i in range(1, got.shape[0]):
        total += got[i]
    rows, batches = sg_all.shape
    total = jnp.concatenate([total[:, :batches], total[:, batches:]], axis=0)
    d_pre = total * sg_all[...]
    both = d_pre[: rows // 2] + d_pre[rows // 2 :]
    hi = both.astype(bf16)
    lo = (both - hi.astype(f32)).astype(bf16)
    g_in[...] = mm(hi, embeds[...]) + mm(lo, embeds[...])
    ones = jnp.ones((1, batches), f32)
    for m in range(2):
        g_mod[m : m + 1, :] = mm_nt(ones, d_pre[m * rows // 2 : (m + 1) * rows // 2], exact)


def give_kernel(base_q, base_vt, out):
    partner = 1 - lax.axis_index("c")
    wq, wv = base_q.shape[1], base_vt.shape[0]
    out[...] = jnp.zeros_like(out)
    for n in range(out.shape[0] // wq):
        at = pl.ds(pl.multiple_of((2 * n + partner) * wq, wq), wq)
        to = slice(n * wq, (n + 1) * wq)
        out[to, :wq] = base_q[at, :]
        out[to, wq : wq + wv] = base_vt[:, at].astype(f32).T.astype(bf16)


def base_kernel(*refs):
    near = refs[:4]
    base_q, base_vt, theirs, acc_q, acc_v, out = refs[4:]
    halves, seqs, length, wq = near[0].shape
    zh, x, c = (lax.axis_index(a) for a in ("zh", "x", "c"))
    nx, nc = len(near), lax.axis_size("c")
    for pair in range(0, nx, 2):
        hs, at, far = [], [], []
        for k in (pair, pair + 1):
            for half in range(halves):
                block = lax.rem(zh + half, halves) * nx + lax.rem(x - k + nx, nx)
                hs.append(near[k][half].reshape(seqs * length, wq))
                at.append(pl.ds(pl.multiple_of((block * nc + c) * wq, wq), wq))
                far.append(pl.ds(pl.multiple_of(block * wq, wq), wq))
        h = jnp.concatenate(hs, axis=1)
        add_q = mm(h, jnp.concatenate([base_q[i, :] for i in at], axis=0))
        add_v = mm_nt(h, jnp.concatenate([base_vt[:, i] for i in at], axis=1))
        partner = mm(h, jnp.concatenate([theirs[i, :] for i in far], axis=0))
        if pair == 0:
            acc_q[...], acc_v[...] = add_q, add_v
            both = partner
        else:
            acc_q[...] += add_q
            acc_v[...] += add_v
            both += partner
    out[...] = both[:, : out.shape[1]].astype(bf16)


def out_kernel(rank, acc_q, acc_v, got, low, ad, q_out, vt_out):
    low = sum_halves(low, rank)
    partner = 1 - lax.axis_index("c")
    seqs, length, wq = q_out.shape
    both = ad[...].astype(f32)
    first = ((0,), (0,))
    for s in range(seqs):
        own = slice(s * length, (s + 1) * length)
        b = both[s * rank : (s + 1) * rank, :].astype(bf16)
        low_q = mm(low[4 * s].astype(bf16), b[:, wq : 2 * wq], first)
        low_v = mm(b[:, 3 * wq :], low[4 * s + 1].astype(bf16), first)
        theirs = got[partner, own, :].astype(f32)
        got_q, got_v = theirs[:, :wq], theirs[:, wq:]
        q_out[s] = (acc_q[own, :] + got_q + scale * low_q).astype(bf16)
        vt_out[s] = ((acc_v[own, :] + got_v).T + scale * low_v).astype(bf16)


def on_device(
    task_embed,
    task_ids,
    seq_lengths,
    w_in,
    module_embed,
    wa_q,
    wb_q,
    wa_v,
    wb_v,
    base_q,
    base_v,
    hidden_in,
    grad_q,
    grad_v,
):
    ny, nz, nh, nx, nc = (lax.axis_size(a) for a in ("y", "zl", "zh", "x", "c"))
    xc, head = ("x", "c"), ("zh", "x", "c")
    seqs, length, wq = hidden_in.shape
    rows, rank, _ = wa_q.shape
    wv = wb_v.shape[2]
    tasks, emb = task_embed.shape
    split, width = 2 * wq, 3 * wq + wv
    batches = seqs * ny * nz
    grad_vt = grad_v.swapaxes(1, 2)

    each = rows * rank // seqs
    id_cols = jnp.broadcast_to(task_ids.astype(bf16)[:, None, None], (seqs, each, 64)).reshape(rows, rank, 64)
    packed = jnp.concatenate([wa_q, wb_q, wa_v, wb_v, id_cols], axis=2).reshape(rows * rank, width + 64)
    w_line = lax.all_gather(packed, "y", axis=0, tiled=True)
    ids_rows = w_line.reshape(ny * seqs, each, width + 64)[:, 0, width].astype(jnp.int32)
    ids_rows = jnp.broadcast_to(ids_rows[None, :, None], (nz, ny * seqs, 128))
    ids_line = swap(ids_rows, "zl")
    lat_line, lat_own, sg_own = local(
        tables_kernel,
        [((2, tasks, ny * rows * rank), bf16), ((2, tasks, rows * rank), bf16), ((2 * rows, tasks), f32)],
        (task_embed, w_in, module_embed),
        name="tables",
    )
    other = lax.ppermute(hidden_in, "zh", [(0, 1), (1, 0)])
    ids_line, w_line, other = lax.optimization_barrier((ids_line, w_line, other))

    (part,) = local(
        functools.partial(part_kernel, split, rank),
        [((nz * seqs * rank, width), bf16)],
        (ids_line, lat_line, w_line),
        name="adapter_parts",
    )
    lat_rows, sg_all, embeds = local(
        functools.partial(batch_kernel, rank),
        [((2, batches * rank, rows * rank), bf16), ((2 * rows, batches), f32), ((batches, emb), bf16)],
        (ids_line, lat_own, sg_own, task_embed),
        name="batch_tables",
    )
    got = swap(part.reshape(nz, seqs * rank, width), "zl")
    got, lat_rows, sg_all, embeds = lax.optimization_barrier((got, lat_rows, sg_all, embeds))
    adapters, low = local(
        functools.partial(low_kernel, wq, wv, rank),
        [((seqs * rank, width), bf16), ((seqs, 2, 2 * rank, length), f32)],
        (seq_lengths, got, hidden_in, grad_q, grad_vt),
        scalars=1,
        name="low_rank",
    )

    low = swap(low.reshape(nx * nc, seqs * 4 * rank // (nx * nc), length), xc)
    low = jnp.sum(low, axis=0).astype(bf16)
    low = spread(low, head, nh * nx * nc)

    blocks = nh * nx
    pair = [(0, 1), (1, 0)]
    base_vt = base_v.T
    (theirs,) = local(
        give_kernel,
        [((blocks * wq, wq + 128), bf16)],
        (base_q, base_vt),
        name="partner_rows",
    )
    theirs = lax.ppermute(theirs, "c", pair)
    low = low.reshape(nh * 4 * seqs * rank, length)
    (d_own,) = local(
        functools.partial(adapter_grad_kernel, wq, wv, rank),
        [((nz, seqs * rank, width + 64), bf16)],
        (seq_lengths, task_ids, low, hidden_in, grad_q, grad_vt),
        scalars=2,
        scratch=[pltpu.VMEM((seqs * rank, width + 64), f32)],
        name="adapter_grads",
    )
    d_line = swap(d_own, "zl").reshape(nz * seqs * rank, width + 64)
    d_all = lax.all_gather(d_line, "y", axis=0, tiled=True)

    both_z = jnp.stack([hidden_in, other])
    turned = [both_z] + [lax.ppermute(both_z, "x", [(i, (i + k) % nx) for i in range(nx)]) for k in range(1, nx)]
    d_all, theirs = lax.optimization_barrier((d_all, theirs))
    acc_q, acc_v, given = local(
        base_kernel,
        [((seqs * length, wq), f32), ((seqs * length, wv), f32), ((seqs * length, wq + wv), bf16)],
        (
            *turned,
            base_q,
            base_vt,
            theirs,
        ),
        mib=20,
        name="base_product",
    )
    (d_lat,) = local(
        functools.partial(latent_grad_kernel, split, width, rank),
        [((nh * nx * nc, rows, 2 * batches), f32)],
        (d_all, packed),
        name="latent_grads",
    )
    d_lat = swap(d_lat, head)
    g_aq, g_bq, g_av, g_bv = local(
        functools.partial(head_grad_kernel, wq, wv),
        [((rows * rank, wq), f32)] * 3 + [((rows * rank, wv), f32)],
        (d_all, lat_rows),
        name="head_grads",
    )
    q_out, vt_out = local(
        functools.partial(out_kernel, rank),
        [((seqs, length, wq), bf16), ((seqs, wv, length), bf16)],
        (acc_q, acc_v, lax.all_gather(given, "c"), low, adapters),
        name="outputs",
    )
    d_lat, g_aq, q_out = lax.optimization_barrier((d_lat, g_aq, q_out))
    g_in, g_mod = local(
        trunk_kernel, [((rows, emb), f32), ((2, rows), f32)], (d_lat, sg_all, embeds), name="trunk_grads"
    )

    def cube(g):
        return g.reshape(rows, rank, -1)

    return (
        q_out,
        vt_out.swapaxes(1, 2),
        cube(g_aq),
        cube(g_bq),
        cube(g_av),
        cube(g_bv),
        g_in.T,
        g_mod,
    )


def solution(mesh):
    fine = Mesh(mesh.devices.reshape(4, 8, 2, 4, 2), ("y", "zl", "zh", "x", "c"))
    dp, head = ("y", "zl"), ("zh", "x", "c")
    rows_cols = P(dp, None, head)
    return jax.shard_map(
        on_device,
        mesh=fine,
        in_specs=(P(), P(dp), P(dp), P(), P())
        + (rows_cols,) * 4
        + (P(None, head),) * 2
        + (rows_cols,) * 3,
        out_specs=(rows_cols,) * 6 + (P(None, dp),) * 2,
        check_vma=False,
    )
```

```python
import functools

import jax
import jax.numpy as jnp
from jax import lax
from jax.experimental import pallas as pl
from jax.experimental.pallas import tpu as pltpu
from jax.sharding import Mesh, PartitionSpec as P

bf16, f32 = jnp.bfloat16, jnp.float32
exact = lax.Precision.HIGHEST
scale = 2.0


def mm(a, b, dims=((1,), (0,)), precision=None):
    return lax.dot_general(a, b, (dims, ((), ())), precision=precision, preferred_element_type=f32)


def mm_nt(a, b, precision=None):
    return mm(a, b, ((1,), (1,)), precision)


def iota(shape, dim):
    return lax.broadcasted_iota(jnp.int32, shape, dim)


def silu_grad(pre):
    sig = jax.nn.sigmoid(pre)
    return sig * (1.0 + pre * (1.0 - sig))


def swap(blocks, axes):
    return lax.all_to_all(blocks, axes, 0, 0, tiled=True)


def spread(block, axes, n):
    return swap(jnp.broadcast_to(block[None], (n,) + block.shape), axes)


def local(body, outs, args, scalars=0, scratch=(), flops=1_000_000, mib=8, name=None):
    in_vmem = pl.BlockSpec(memory_space=pltpu.VMEM)
    in_smem = pl.BlockSpec(memory_space=pltpu.SMEM)
    return pl.pallas_call(
        body,
        out_shape=tuple(jax.ShapeDtypeStruct(s, d) for s, d in outs),
        in_specs=[in_smem] * scalars + [in_vmem] * (len(args) - scalars),
        out_specs=tuple(in_vmem for _ in outs),
        scratch_shapes=list(scratch),
        compiler_params=pltpu.CompilerParams(vmem_limit_bytes=mib * 2**20),
        cost_estimate=pl.CostEstimate(flops=flops, bytes_accessed=100_000, transcendentals=0),
        name=name,
    )(*args)


def tables_kernel(task_embed, w_in, module, lat_line, lat_own, sg_own):
    ny, nz = lax.axis_size("y"), lax.axis_size("zl")
    latents = w_in.shape[1]
    rows = latents // (ny * nz)
    rank = lat_own.shape[2] // rows
    y, z = lax.axis_index("y"), lax.axis_index("zl")
    pre = mm(task_embed[...], w_in[...])
    q = iota((latents, lat_line.shape[2]), 1)
    line = iota((latents, lat_line.shape[2]), 0) == (
        (q // (rows * rank)) * (nz * rows) + z * rows + (q // rank) % rows
    )
    line = line.astype(f32).astype(bf16)
    first = (y * nz + z) * rows
    q = iota((latents, lat_own.shape[2]), 1)
    own = (iota((latents, lat_own.shape[2]), 0) == first + q // rank).astype(f32).astype(bf16)
    mine = (iota((rows, latents), 1) == first + iota((rows, latents), 0)).astype(f32)
    for m in range(2):
        p = pre + module[m : m + 1, :]
        lat = (p * jax.nn.sigmoid(p)).astype(bf16)
        lat_line[m] = mm(lat, line).astype(bf16)
        lat_own[m] = mm(lat, own).astype(bf16)
        sg_own[m * rows : (m + 1) * rows, :] = mm_nt(mine, silu_grad(p), exact)


def pick_tasks(ids, tasks):
    at = ids[...].reshape(ids.shape[0] * ids.shape[1], ids.shape[2])[:, :1]
    return (iota((at.shape[0], tasks), 1) == at).astype(f32).astype(bf16)


def batch_kernel(rank, ids, lat_own, sg_own, task_embed, lat_rows, sg_all, embeds):
    of_all = pick_tasks(ids, lat_own.shape[1])
    ny, nz = lax.axis_size("y"), lax.axis_size("zl")
    batches = of_all.shape[0]
    seqs = batches // (ny * nz)

    def ordered(repeat):
        i, j = iota((batches * repeat, batches), 0) // repeat, iota((batches * repeat, batches), 1)
        hit = (i // (nz * seqs) == (j // seqs) % ny) & ((i // seqs) % nz == j // (seqs * ny)) & (i % seqs == j % seqs)
        return mm(hit.astype(f32).astype(bf16), of_all)

    n, k = lat_rows.shape[1:]
    pick = ordered(rank).astype(bf16)
    same = iota((n, k), 0) % rank == iota((n, k), 1) % rank
    for m in range(2):
        lat_rows[m] = jnp.where(same, mm(pick, lat_own[m]), 0.0).astype(bf16)
    one = ordered(1)
    sg_all[...] = mm_nt(sg_own[...], one, exact)
    embeds[...] = mm(one.astype(bf16), task_embed[...]).astype(bf16)


def part_kernel(split, rank, ids, lat_line, w_line, part):
    n, k = part.shape[0], w_line.shape[0]
    of_all = pick_tasks(ids, lat_line.shape[1])
    i, j = iota((n, of_all.shape[0]), 0), iota((n, of_all.shape[0]), 1)
    ny, y = lax.axis_size("y"), lax.axis_index("y")
    seqs = ids.shape[1] // ny
    mine = (i // (seqs * rank) == j // (seqs * ny)) & ((i // rank) % seqs == j % seqs) & ((j // seqs) % ny == y)
    pick = mm(mine.astype(f32).astype(bf16), of_all).astype(bf16)
    same = iota((n, k), 0) % rank == iota((n, k), 1) % rank
    for m, cols in enumerate((slice(0, split), slice(split, part.shape[1]))):
        spread_lat = jnp.where(same, mm(pick, lat_line[m]), 0.0).astype(bf16)
        part[:, cols] = mm(spread_lat, w_line[:, cols]).astype(bf16)


def row_weight(lengths, s, length):
    n = jnp.full((1, length), lengths[s], jnp.int32)
    return jnp.where(iota((1, length), 1) < n, scale / n.astype(f32), 0.0)


def low_kernel(wq, wv, rank, lengths, got, hidden, grad_q, grad_vt, adapters, low):
    total = got[0].astype(f32)
    for i in range(1, got.shape[0]):
        total += got[i].astype(f32)
    adapters[...] = total.astype(bf16)
    total = total.astype(bf16).astype(f32)
    for s in range(hidden.shape[0]):
        own = total[s * rank : (s + 1) * rank, :]
        a = jnp.concatenate([own[:, :wq], own[:, 2 * wq : 3 * wq]], axis=0).astype(bf16)
        b_q, b_v = own[:, wq : 2 * wq].astype(bf16), own[:, 3 * wq :].astype(bf16)
        low[s, 0] = mm_nt(a, hidden[s]).astype(low.dtype)
        back = jnp.concatenate([mm_nt(b_q, grad_q[s]), mm(b_v, grad_vt[s])], axis=0)
        low[s, 1] = (back * row_weight(lengths, s, hidden.shape[1])).astype(low.dtype)


def sum_halves(low, rank):
    both = low[...].astype(f32)
    rows = both.shape[0] // 2
    return (both[:rows] + both[rows:]).reshape(rows // rank, rank, both.shape[1])


def adapter_grad_kernel(wq, wv, rank, lengths, ids, low, hidden, grad_q, grad_vt, out, rows):
    low = sum_halves(low, rank)
    for s in range(hidden.shape[0]):
        at = slice(s * rank, (s + 1) * rank)
        weight = row_weight(lengths, s, hidden.shape[1])
        du = jnp.concatenate([low[4 * s + 2], low[4 * s + 3]], axis=0).astype(bf16)
        d_a = mm(du, hidden[s])
        rows[at, :wq] = d_a[:rank]
        rows[at, wq : 2 * wq] = mm((low[4 * s] * weight).astype(bf16), grad_q[s])
        rows[at, 2 * wq : 3 * wq] = d_a[rank:]
        rows[at, 3 * wq : 3 * wq + wv] = mm_nt((low[4 * s + 1] * weight).astype(bf16), grad_vt[s])
        rest = rows.shape[1] - 3 * wq - wv
        rows[at, 3 * wq + wv :] = jnp.full((rank, rest), ids[s], jnp.int32).astype(f32)
    done = rows[...].astype(bf16)
    for i in range(out.shape[0]):
        out[i] = done


def latent_grad_kernel(split, width, rank, d_all, weights, out):
    n, k = d_all.shape[0], weights.shape[0]
    same = iota((n, k), 0) % rank == iota((n, k), 1) % rank
    fold = (iota((k // rank, k), 0) == iota((k // rank, k), 1) // rank).astype(f32)
    parts = []
    for cols in (slice(0, split), slice(split, width)):
        full = jnp.where(same, mm_nt(d_all[:, cols], weights[:, cols]), 0.0)
        by_batch = jnp.sum(full.reshape(n // rank, rank, k), axis=1)
        parts.append(mm_nt(fold, by_batch, exact))
    both = jnp.concatenate(parts, axis=1).astype(out.dtype)
    for i in range(out.shape[0]):
        out[i] = both


def head_grad_kernel(wq, wv, d_all, lat_rows, g_aq, g_bq, g_av, g_bv):
    width = 3 * wq + wv
    g_q = mm(lat_rows[0], d_all[:, : 2 * wq], ((0,), (0,)))
    g_aq[...], g_bq[...] = g_q[:, :wq], g_q[:, wq:]
    g_v = mm(lat_rows[1], d_all[:, 2 * wq : width], ((0,), (0,)))
    g_av[...], g_bv[...] = g_v[:, :wq], g_v[:, wq:]


def trunk_kernel(got, sg_all, embeds, g_in, g_mod):
    total = got[0].astype(f32)
    for i in range(1, got.shape[0]):
        total += got[i].astype(f32)
    rows, batches = sg_all.shape
    total = jnp.concatenate([total[:, :batches], total[:, batches:]], axis=0)
    d_pre = total * sg_all[...]
    both = d_pre[: rows // 2] + d_pre[rows // 2 :]
    hi = both.astype(bf16)
    lo = (both - hi.astype(f32)).astype(bf16)
    g_in[...] = mm(hi, embeds[...]) + mm(lo, embeds[...])
    ones = jnp.ones((1, batches), f32)
    for m in range(2):
        g_mod[m : m + 1, :] = mm_nt(ones, d_pre[m * rows // 2 : (m + 1) * rows // 2], exact)


def give_kernel(base_q, base_vt, out):
    partner = 1 - lax.axis_index("c")
    wq, wv = base_q.shape[1], base_vt.shape[0]
    out[...] = jnp.zeros_like(out)
    for n in range(out.shape[0] // wq):
        at = pl.ds(pl.multiple_of((2 * n + partner) * wq, wq), wq)
        to = slice(n * wq, (n + 1) * wq)
        out[to, :wq] = base_q[at, :]
        out[to, wq : wq + wv] = base_vt[:, at].astype(f32).T.astype(bf16)


def base_kernel(*refs):
    near = refs[:4]
    base_q, base_vt, theirs, acc_q, acc_v, out = refs[4:]
    halves, seqs, length, wq = near[0].shape
    zh, x, c = (lax.axis_index(a) for a in ("zh", "x", "c"))
    nx, nc = len(near), lax.axis_size("c")
    for pair in range(0, nx, 2):
        hs, at, far = [], [], []
        for k in (pair, pair + 1):
            for half in range(halves):
                block = lax.rem(zh + half, halves) * nx + lax.rem(x - k + nx, nx)
                hs.append(near[k][half].reshape(seqs * length, wq))
                at.append(pl.ds(pl.multiple_of((block * nc + c) * wq, wq), wq))
                far.append(pl.ds(pl.multiple_of(block * wq, wq), wq))
        h = jnp.concatenate(hs, axis=1)
        add_q = mm(h, jnp.concatenate([base_q[i, :] for i in at], axis=0))
        add_v = mm_nt(h, jnp.concatenate([base_vt[:, i] for i in at], axis=1))
        partner = mm(h, jnp.concatenate([theirs[i, :] for i in far], axis=0))
        if pair == 0:
            acc_q[...], acc_v[...] = add_q, add_v
            both = partner
        else:
            acc_q[...] += add_q
            acc_v[...] += add_v
            both += partner
    out[...] = both[:, : out.shape[1]].astype(bf16)


def out_kernel(rank, acc_q, acc_v, got, low, ad, q_out, vt_out):
    low = sum_halves(low, rank)
    partner = 1 - lax.axis_index("c")
    seqs, length, wq = q_out.shape
    both = ad[...].astype(f32)
    first = ((0,), (0,))
    for s in range(seqs):
        own = slice(s * length, (s + 1) * length)
        b = both[s * rank : (s + 1) * rank, :].astype(bf16)
        low_q = mm(low[4 * s].astype(bf16), b[:, wq : 2 * wq], first)
        low_v = mm(b[:, 3 * wq :], low[4 * s + 1].astype(bf16), first)
        theirs = got[partner, own, :].astype(f32)
        got_q, got_v = theirs[:, :wq], theirs[:, wq:]
        q_out[s] = (acc_q[own, :] + got_q + scale * low_q).astype(bf16)
        vt_out[s] = ((acc_v[own, :] + got_v).T + scale * low_v).astype(bf16)


def on_device(
    task_embed,
    task_ids,
    seq_lengths,
    w_in,
    module_embed,
    wa_q,
    wb_q,
    wa_v,
    wb_v,
    base_q,
    base_v,
    hidden_in,
    grad_q,
    grad_v,
):
    ny, nz, nh, nx, nc = (lax.axis_size(a) for a in ("y", "zl", "zh", "x", "c"))
    xc, head = ("x", "c"), ("zh", "x", "c")
    seqs, length, wq = hidden_in.shape
    rows, rank, _ = wa_q.shape
    wv = wb_v.shape[2]
    tasks, emb = task_embed.shape
    split, width = 2 * wq, 3 * wq + wv
    batches = seqs * ny * nz
    grad_vt = grad_v.swapaxes(1, 2)

    each = rows * rank // seqs
    id_cols = jnp.broadcast_to(task_ids.astype(bf16)[:, None, None], (seqs, each, 64)).reshape(rows, rank, 64)
    packed = jnp.concatenate([wa_q, wb_q, wa_v, wb_v, id_cols], axis=2).reshape(rows * rank, width + 64)
    w_line = lax.all_gather(packed, "y", axis=0, tiled=True)
    ids_rows = w_line.reshape(ny * seqs, each, width + 64)[:, 0, width].astype(jnp.int32)
    ids_rows = jnp.broadcast_to(ids_rows[None, :, None], (nz, ny * seqs, 128))
    ids_line = swap(ids_rows, "zl")
    lat_line, lat_own, sg_own = local(
        tables_kernel,
        [((2, tasks, ny * rows * rank), bf16), ((2, tasks, rows * rank), bf16), ((2 * rows, tasks), f32)],
        (task_embed, w_in, module_embed),
        name="tables",
    )
    other = lax.ppermute(hidden_in, "zh", [(0, 1), (1, 0)])
    ids_line, w_line, other = lax.optimization_barrier((ids_line, w_line, other))

    (part,) = local(
        functools.partial(part_kernel, split, rank),
        [((nz * seqs * rank, width), bf16)],
        (ids_line, lat_line, w_line),
        name="adapter_parts",
    )
    lat_rows, sg_all, embeds = local(
        functools.partial(batch_kernel, rank),
        [((2, batches * rank, rows * rank), bf16), ((2 * rows, batches), f32), ((batches, emb), bf16)],
        (ids_line, lat_own, sg_own, task_embed),
        name="batch_tables",
    )
    got = swap(part.reshape(nz, seqs * rank, width), "zl")
    got, lat_rows, sg_all, embeds = lax.optimization_barrier((got, lat_rows, sg_all, embeds))
    adapters, low = local(
        functools.partial(low_kernel, wq, wv, rank),
        [((seqs * rank, width), bf16), ((seqs, 2, 2 * rank, length), bf16)],
        (seq_lengths, got, hidden_in, grad_q, grad_vt),
        scalars=1,
        name="low_rank",
    )

    low = swap(low.reshape(nx * nc, seqs * 4 * rank // (nx * nc), length), xc)
    low = jnp.sum(low.astype(f32), axis=0).astype(bf16)
    low = spread(low, head, nh * nx * nc)

    blocks = nh * nx
    pair = [(0, 1), (1, 0)]
    base_vt = base_v.T
    (theirs,) = local(
        give_kernel,
        [((blocks * wq, wq + 128), bf16)],
        (base_q, base_vt),
        name="partner_rows",
    )
    theirs = lax.ppermute(theirs, "c", pair)
    low = low.reshape(nh * 4 * seqs * rank, length)
    (d_own,) = local(
        functools.partial(adapter_grad_kernel, wq, wv, rank),
        [((nz, seqs * rank, width + 64), bf16)],
        (seq_lengths, task_ids, low, hidden_in, grad_q, grad_vt),
        scalars=2,
        scratch=[pltpu.VMEM((seqs * rank, width + 64), f32)],
        name="adapter_grads",
    )
    d_line = swap(d_own, "zl").reshape(nz * seqs * rank, width + 64)
    d_all = lax.all_gather(d_line, "y", axis=0, tiled=True)

    both_z = jnp.stack([hidden_in, other])
    turned = [both_z] + [lax.ppermute(both_z, "x", [(i, (i + k) % nx) for i in range(nx)]) for k in range(1, nx)]
    d_all, theirs = lax.optimization_barrier((d_all, theirs))
    acc_q, acc_v, given = local(
        base_kernel,
        [((seqs * length, wq), f32), ((seqs * length, wv), f32), ((seqs * length, wq + wv), bf16)],
        (
            *turned,
            base_q,
            base_vt,
            theirs,
        ),
        mib=20,
        name="base_product",
    )
    (d_lat,) = local(
        functools.partial(latent_grad_kernel, split, width, rank),
        [((nh * nx * nc, rows, 2 * batches), bf16)],
        (d_all, packed),
        name="latent_grads",
    )
    d_lat = swap(d_lat, head)
    g_aq, g_bq, g_av, g_bv = local(
        functools.partial(head_grad_kernel, wq, wv),
        [((rows * rank, wq), f32)] * 3 + [((rows * rank, wv), f32)],
        (d_all, lat_rows),
        name="head_grads",
    )
    q_out, vt_out = local(
        functools.partial(out_kernel, rank),
        [((seqs, length, wq), bf16), ((seqs, wv, length), bf16)],
        (acc_q, acc_v, lax.all_gather(given, "c"), low, adapters),
        name="outputs",
    )
    d_lat, g_aq, q_out = lax.optimization_barrier((d_lat, g_aq, q_out))
    g_in, g_mod = local(
        trunk_kernel, [((rows, emb), f32), ((2, rows), f32)], (d_lat, sg_all, embeds), name="trunk_grads"
    )

    def cube(g):
        return g.reshape(rows, rank, -1)

    return (
        q_out,
        vt_out.swapaxes(1, 2),
        cube(g_aq),
        cube(g_bq),
        cube(g_av),
        cube(g_bv),
        g_in.T,
        g_mod,
    )


def solution(mesh):
    fine = Mesh(mesh.devices.reshape(4, 8, 2, 4, 2), ("y", "zl", "zh", "x", "c"))
    dp, head = ("y", "zl"), ("zh", "x", "c")
    rows_cols = P(dp, None, head)
    return jax.shard_map(
        on_device,
        mesh=fine,
        in_specs=(P(), P(dp), P(dp), P(), P())
        + (rows_cols,) * 4
        + (P(None, head),) * 2
        + (rows_cols,) * 3,
        out_specs=(rows_cols,) * 6 + (P(None, dp),) * 2,
        check_vma=False,
    )
```
